32 devices in a mesh: row: 4 (over z), col: 8 (over y, x, core).
Axes of the slice: x: 2, y: 2, z: 4, core: 2. Of those that a mesh axis runs over, the one named last changes fastest.
Arguments:
- features: bfloat16 [8192, 512], P(('row', 'col')), may hold values from -6 to 6
- cotangent: bfloat16 [8192, 512], P(('row', 'col')), may hold values from -6 to 6
- weights: bfloat16 [512, 512], replicated, may hold values from -0.25 to 0.25
- bias_term: float32 [512], replicated, may hold values from -3 to 3
- adjacency: bfloat16 [4, 8, 128, 128, 128], P('row', 'col'), may hold values from -0.109375 to 0.109375
- tile_rows: int32 [4, 8, 128], P('row', 'col'), may hold values from 0 to 15, as said below
- tile_cols: int32 [4, 8, 128], P('row', 'col'), may hold values from 0 to 7
- tile_count: int32 [4, 8], P('row', 'col'), may hold values from 25 to 128, as said below
Outputs:
- activated: bfloat16 [8192, 512], P(('row', 'col'))
- grad_input: bfloat16 [8192, 512], P(('row', 'col'))
- grad_weight: float32 [512, 512], replicated
- grad_bias: float32 [512], replicated
The draws below stay inside these ranges and needn't reach their ends.
Inputs may be any that keep to these rules, and one draw needn't show every extreme that they name: Within one device the pairs (tile_rows, tile_cols) over all 128 slots are distinct. Only the first tile_count slots of a device are in use; some device uses all 128.
All inputs are finite; a program needn't handle non-finite values.
Results may differ from the reference program's by a relative error of at most 0.006.
Values may be sent and summed in bfloat16 or wider, within the bound.
A program may use at most 128 MiB of HBM per device.

```python
import jax
import jax.numpy as jnp
from jax import lax

F = 512
TILE = 128
BPD = 2
TILE_CAP = 128
NODES = 8192
N_ROW = 4
N_COL = 8


def tile_pairs(key):
    pair_total = N_COL * BPD * N_ROW * BPD
    keys = jax.random.split(jax.random.fold_in(key, 11), N_ROW * N_COL)
    chosen = jax.vmap(lambda one_key: jax.random.permutation(one_key, pair_total)[:TILE_CAP])(keys)
    return chosen.reshape(N_ROW, N_COL, TILE_CAP).astype(jnp.int32)


def draw_tile_rows(key, part):
    return (tile_pairs(key) // (N_ROW * BPD)).astype(jnp.int32)


def draw_tile_cols(key, part):
    return (tile_pairs(key) % (N_ROW * BPD)).astype(jnp.int32)


def draw_tile_count(key, part):
    first_key = jax.random.fold_in(key, 23)
    second_key = jax.random.fold_in(key, 29)
    dev_total = N_ROW * N_COL
    low_count = max(1, TILE_CAP // 5)
    base_count = jax.random.randint(first_key, (dev_total,), low_count, TILE_CAP // 2 + 1, dtype=jnp.int32)
    busiest = jax.random.randint(second_key, (), 0, dev_total, dtype=jnp.int32)
    lightest = ((busiest + 1) % dev_total).astype(jnp.int32)
    base_count = base_count.at[lightest].set(low_count)
    base_count = base_count.at[busiest].set(TILE_CAP)
    return base_count.reshape(N_ROW, N_COL).astype(jnp.int32)


def level_of(own_key, shape, cuts, low, high):
    factor_of = 1.0
    for dim, parts in cuts:
        heights = jax.random.uniform(jax.random.fold_in(jax.random.fold_in(own_key, 6), dim), (parts,), jnp.float32, low / len(cuts), high / len(cuts))
        factor_of = factor_of * jnp.repeat(jnp.exp(heights), shape[dim] // parts).reshape((-1,) + (1,) * (len(shape) - 1 - dim))
    return factor_of


def bell_draw(own_key, shape, width, bound, pieces=(), kind=jnp.bfloat16):
    values = jax.random.normal(own_key, shape, jnp.float32) * width
    if len(pieces) > 0:
        values = level_of(own_key, shape, pieces, -0.22, 0.18) * values
    return jnp.clip(values, min=-bound, max=bound).astype(kind)


def setup_inputs(seed: int = 0) -> dict:
    streams_of = jax.random.split(jax.random.key(seed), 9)
    features = bell_draw(streams_of[0], (NODES, F), 1.0, 6.0, ((0, 32),))
    cotangent = bell_draw(streams_of[1], (NODES, F), 1.0, 6.0, ((0, 32),))
    weights = bell_draw(streams_of[2], (F, F), F ** -0.5, 0.25)
    bias_term = bell_draw(streams_of[3], (F,), 0.5, 3.0, (), jnp.float32)
    adjacency = bell_draw(streams_of[4], (N_ROW, N_COL, TILE_CAP, TILE, TILE), (TILE * TILE_CAP // (3 * BPD)) ** -0.5, 0.109375, ((0, 4), (1, 8)))
    tile_rows = draw_tile_rows(jax.random.fold_in(streams_of[8], 71), 0)
    tile_cols = draw_tile_cols(jax.random.fold_in(streams_of[8], 71), 0)
    tile_count = draw_tile_count(jax.random.fold_in(streams_of[8], 71), 0)
    return {"features": features, "cotangent": cotangent, "weights": weights, "bias_term": bias_term, "adjacency": adjacency, "tile_rows": tile_rows, "tile_cols": tile_cols, "tile_count": tile_count}


def global_ids(grid_row, grid_col, tile_rows, tile_cols):
    row_piece = grid_row * N_COL + tile_rows // BPD
    col_piece = (tile_cols // BPD) * N_COL + grid_col
    row_block = row_piece * BPD + tile_rows % BPD
    col_block = col_piece * BPD + tile_cols % BPD
    return row_block.astype(jnp.int32), col_block.astype(jnp.int32)


def reference(features, cotangent, weights, bias_term, adjacency, tile_rows, tile_cols, tile_count):
    block_total = NODES // TILE
    dev_total = N_ROW * N_COL
    grid_row = (jnp.arange(dev_total, dtype=jnp.int32) // N_COL).astype(jnp.int32)
    grid_col = (jnp.arange(dev_total, dtype=jnp.int32) % N_COL).astype(jnp.int32)
    flat_tiles = adjacency.reshape(dev_total, TILE_CAP, TILE, TILE)
    flat_rows = tile_rows.reshape(dev_total, TILE_CAP)
    flat_cols = tile_cols.reshape(dev_total, TILE_CAP)
    flat_count = tile_count.reshape(dev_total)
    slot_index = jnp.arange(TILE_CAP, dtype=jnp.int32)

    projected = jnp.dot(features, weights, preferred_element_type=jnp.float32).astype(jnp.bfloat16)
    proj_blocks = projected.reshape(block_total, TILE, F)

    def forward_step(carry, inputs):
        tile_data, rows_here, cols_here, count_here, row_here, col_here = inputs
        row_block, col_block = global_ids(row_here, col_here, rows_here, cols_here)
        in_use = (slot_index < count_here).astype(jnp.float32)
        picked = proj_blocks[col_block].astype(jnp.float32)
        products = jnp.einsum("tij,tjf->tif", tile_data.astype(jnp.float32), picked)
        products = products * in_use[:, None, None]
        return carry.at[row_block].add(products), None

    start_blocks = jnp.zeros((block_total, TILE, F), jnp.float32)
    summed, _ = lax.scan(forward_step, start_blocks, (flat_tiles, flat_rows, flat_cols, flat_count, grid_row, grid_col))
    summed = summed.reshape(NODES, F)
    shifted = summed + bias_term[None, :]
    activated = jax.nn.silu(shifted).astype(jnp.bfloat16)
    sig = jax.nn.sigmoid(shifted)
    slope = (cotangent.astype(jnp.float32) * sig * (1.0 + shifted * (1.0 - sig))).astype(jnp.bfloat16)
    slope_blocks = slope.reshape(block_total, TILE, F)

    def backward_step(carry, inputs):
        tile_data, rows_here, cols_here, count_here, row_here, col_here = inputs
        row_block, col_block = global_ids(row_here, col_here, rows_here, cols_here)
        in_use = (slot_index < count_here).astype(jnp.float32)
        picked = slope_blocks[row_block].astype(jnp.float32)
        products = jnp.einsum("tji,tjf->tif", tile_data.astype(jnp.float32), picked)
        products = products * in_use[:, None, None]
        return carry.at[col_block].add(products), None

    back, _ = lax.scan(backward_step, start_blocks, (flat_tiles, flat_rows, flat_cols, flat_count, grid_row, grid_col))
    back = back.reshape(NODES, F).astype(jnp.bfloat16)
    grad_input = jnp.dot(back, weights.T, preferred_element_type=jnp.float32).astype(jnp.bfloat16)
    node_scale = NODES ** -0.5
    grad_weight = jnp.dot(features.T, back, preferred_element_type=jnp.float32) * node_scale
    grad_bias = jnp.sum(slope.astype(jnp.float32), axis=0) * node_scale
    return activated, grad_input, grad_weight, grad_bias
```

```python
import functools
import math

import jax
import jax.numpy as jnp
from jax import lax
from jax.experimental import pallas as pl
from jax.experimental.pallas import tpu as pltpu
from jax.sharding import PartitionSpec as P

MESH = pl.DeviceIdType.MESH
NCH = 4


def kernel(
    R, C, tile, cap, scale,
    feat, cot, w_ref, bias, inv, adj_hbm,
    act, gin, gw, gb,
    adj_v, A, proj, s1, r1, p1, s2, r2, ST, pc, sbR, sbL, rsR, rsL, XT, bp, gacc,
    wsend, wrecv, zsum, fin,
    adj_sem, zrs, zrr, zls, zlr, c1s, c1r, c2s, c2r, ags, agr, ocs, ocr,
    rrs, rrr, rls, rlr, wss, wsr, zss, zsr, fns, fnr,
):
    B, F = feat.shape
    w = F // NCH
    Q = C // 2
    RW = F // C
    K = B // tile
    z = lax.axis_index("row")
    c = lax.axis_index("col")
    core = lax.rem(c, 2)
    q = c // 2
    partner = (z, q * 2 + 1 - core)

    def at_q(d):
        return (z, lax.rem(q + d, Q) * 2 + core)

    def at_c(e):
        return (z, lax.rem(c + e, C))

    def at_z(e):
        return (lax.rem(z + e, R), c)

    adj_copy = pltpu.make_async_copy(adj_hbm, adj_v.at[pl.ds(0, cap)], adj_sem)
    adj_copy.start()

    barrier = pltpu.get_barrier_semaphore()
    for e in range(1, C):
        pl.semaphore_signal(barrier, inc=1, device_id=at_c(e), device_id_type=MESH)
    for e in range(1, R):
        pl.semaphore_signal(barrier, inc=1, device_id=at_z(e), device_id_type=MESH)

    def rcopy(src, dst, ss, rs, dev):
        return pltpu.make_async_remote_copy(
            src_ref=src, dst_ref=dst, send_sem=ss, recv_sem=rs, device_id=dev, device_id_type=MESH
        )

    def z_right(k, m, slot):
        return rcopy(proj.at[k, slot], proj.at[k, slot], zrs.at[k, m], zrr.at[k, m], (lax.rem(z + 1, R), c))

    def z_left(k, m, slot):
        return rcopy(proj.at[k, slot], proj.at[k, slot], zls.at[k, m], zlr.at[k, m], (lax.rem(z + R - 1, R), c))

    def core_sum(k):
        return rcopy(s1.at[k], r1.at[k], c1s.at[k], c1r.at[k], partner)

    def chip_sum(k, d):
        return rcopy(s2.at[k, d], r2.at[k, d], c2s.at[k, d], c2r.at[k, d], at_q(d))

    def slope_chip(k, d, slot):
        return rcopy(ST.at[k, slot], ST.at[k, slot], ags.at[k, d], agr.at[k, d], at_q(d))

    def slope_core(k, d, slot):
        return rcopy(ST.at[k, slot], ST.at[k, slot], ocs.at[k, d], ocr.at[k, d], partner)

    def back_right(k, t):
        return rcopy(sbR.at[k, t], rsR.at[k, t], rrs.at[k, t], rrr.at[k, t], (lax.rem(z + 1, R), c))

    def back_left(k, t):
        return rcopy(sbL.at[k, t], rsL.at[k, t], rls.at[k, t], rlr.at[k, t], (lax.rem(z + R - 1, R), c))

    def weight_part(k, e, src, slot):
        return rcopy(wsend.at[k, src], wrecv.at[k, slot], wss.at[k, e], wsr.at[k, e], at_c(e))

    def weight_z(k, e, slot):
        return rcopy(zsum.at[k, slot], zsum.at[k, slot], zss.at[k, e], zsr.at[k, e], at_z(e))

    def weight_all(k, e, slot):
        return rcopy(fin.at[k, slot], fin.at[k, slot], fns.at[k, e], fnr.at[k, e], at_c(e))

    def cols(k):
        return pl.ds(pl.multiple_of(k * w, w), w)

    full = jnp.dot(feat[...], w_ref[...], preferred_element_type=jnp.float32).astype(jnp.bfloat16)
    for k in range(NCH):
        proj[k, z] = full[:, k * w:(k + 1) * w]
    pl.semaphore_wait(barrier, C + R - 2)

    def send_own(k):
        @pl.when(z + 1 < R)
        def _():
            z_right(k, 0, z).start()

        @pl.when(z >= 1)
        def _():
            z_left(k, 0, z).start()

    send_own(0)
    XT[...] = feat[...].astype(jnp.float32).T.astype(jnp.bfloat16)
    gacc[...] = jnp.zeros_like(gacc)
    adj_v[cap] = jnp.zeros((tile, tile), jnp.bfloat16)
    adj_copy.wait()

    @pl.loop(0, C * K)
    def _(rb):
        for cb in range(R * K):
            A[pl.ds(pl.multiple_of(rb * tile, tile), tile), cb * tile:(cb + 1) * tile] = adj_v[
                inv[rb * (R * K) + cb]
            ]

    def relay(k, m):
        @pl.when(z - 1 - m >= 0)
        def _():
            slot = lax.rem(z - 1 - m + R, R)
            z_right(k, m, slot).wait_recv()
            if m + 1 < R - 1:
                @pl.when(z + 1 < R)
                def _():
                    z_right(k, m + 1, slot).start()

        @pl.when(z + 1 + m < R)
        def _():
            slot = lax.rem(z + 1 + m, R)
            z_left(k, m, slot).wait_recv()
            if m + 1 < R - 1:
                @pl.when(z >= 1)
                def _():
                    z_left(k, m + 1, slot).start()

    def forward(k):
        source = proj[k].reshape(R * B, w)

        def rows_of(c2):
            return A[pl.ds(pl.multiple_of(c2 * B, B), B), :]

        @pl.loop(0, Q)
        def _(j):
            s1[k, j] = jnp.dot(
                rows_of(2 * j + 1 - core), source, preferred_element_type=jnp.float32
            ).astype(jnp.bfloat16)

        core_sum(k).start()

        @pl.loop(0, Q)
        def _(j):
            p1[k, j] = jnp.dot(rows_of(2 * j + core), source, preferred_element_type=jnp.float32)

    def chip_send(k):
        core_sum(k).wait_recv()
        for d in range(1, Q):
            j = lax.rem(q + d, Q)
            s2[k, d] = (p1[k, j] + r1[k, j].astype(jnp.float32)).astype(jnp.bfloat16)
            chip_sum(k, d).start()

    def activate(k):
        total = p1[k, q] + r1[k, q].astype(jnp.float32)
        for d in range(1, Q):
            chip_sum(k, d).wait_recv()
            total = total + r2[k, d].astype(jnp.float32)
        shifted = total + bias[:, cols(k)]
        sig = jax.nn.sigmoid(shifted)
        slope = cot[:, cols(k)].astype(jnp.float32) * sig * (1.0 + shifted * (1.0 - sig))
        slope = slope.astype(jnp.bfloat16).astype(jnp.float32)
        ST[k, c] = slope.T.astype(jnp.bfloat16)
        for d in range(1, Q):
            slope_chip(k, d, c).start()
        slope_core(k, 0, c).start()
        act[:, cols(k)] = (shifted * sig).astype(jnp.bfloat16)
        bp[k] = jnp.sum(slope, axis=0, keepdims=True)

    def backward(k):
        for d in range(1, Q):
            slot = lax.rem(q - d + Q, Q) * 2 + core
            slope_chip(k, d, slot).wait_recv()
            slope_core(k, d, slot).start()
        for d in range(Q):
            slot = lax.rem(q - d + Q, Q) * 2 + 1 - core
            slope_core(k, d, slot).wait_recv()

        @pl.loop(0, R)
        def _(t):
            acc = jnp.zeros((w, B), jnp.float32)
            for j in range(C):
                acc = acc + jnp.dot(
                    ST[k, j],
                    A[j * B:(j + 1) * B, pl.ds(pl.multiple_of(t * B, B), B)],
                    preferred_element_type=jnp.float32,
                )
            pc[k, t] = acc

    def back_sum(k):
        for j in range(R - 1):
            t = R - 1 - j

            @pl.when((z >= 1) & (z <= t))
            def _():
                back_right(k, t).wait_recv()

            @pl.when((z >= 1) & (z < t))
            def _():
                sbR[k, t] = (pc[k, t] + rsR[k, t].astype(jnp.float32)).astype(jnp.bfloat16)

            @pl.when(z == 0)
            def _():
                sbR[k, t] = pc[k, t].astype(jnp.bfloat16)

            @pl.when(z < t)
            def _():
                back_right(k, t).start()

            u = j

            @pl.when((z < R - 1) & (z >= u))
            def _():
                back_left(k, u).wait_recv()

            @pl.when((z < R - 1) & (z > u))
            def _():
                sbL[k, u] = (pc[k, u] + rsL[k, u].astype(jnp.float32)).astype(jnp.bfloat16)

            @pl.when(z == R - 1)
            def _():
                sbL[k, u] = pc[k, u].astype(jnp.bfloat16)

            @pl.when(z > u)
            def _():
                back_left(k, u).start()

    def finish(k):
        @pl.when(z >= 1)
        def _():
            pc[k, z] = pc[k, z] + rsR[k, z].astype(jnp.float32)

        @pl.when(z < R - 1)
        def _():
            pc[k, z] = pc[k, z] + rsL[k, z].astype(jnp.float32)

        back = pc[k, z].T.astype(jnp.bfloat16)
        part = jnp.dot(XT[...], back, preferred_element_type=jnp.float32)
        wsend[k, :, 0:RW, :] = part.astype(jnp.bfloat16).reshape(C, RW, w)
        wsend[k, :, RW:RW + 16, :] = jnp.broadcast_to(bp[k].astype(jnp.bfloat16)[None], (C, 16, w))
        for e in range(1, C):
            weight_part(k, e, lax.rem(c + e, C), c).start()
        wrecv[k, c] = wsend[k, c]
        gacc[...] += lax.dot_general(
            back, w_ref[:, cols(k)], (((1,), (1,)), ((), ())), preferred_element_type=jnp.float32
        )

    def weight_sum(k):
        for e in range(1, C):
            weight_part(k, e, 0, lax.rem(c - e + C, C)).wait_recv()
        total = wrecv[k, 0].astype(jnp.float32)
        for j in range(1, C):
            total = total + wrecv[k, j].astype(jnp.float32)
        zsum[k, z] = total.astype(jnp.bfloat16)
        for e in range(1, R):
            weight_z(k, e, z).start()

    def weight_total(k):
        for e in range(1, R):
            weight_z(k, e, lax.rem(z - e + R, R)).wait_recv()
        total = zsum[k, 0].astype(jnp.float32)
        for j in range(1, R):
            total = total + zsum[k, j].astype(jnp.float32)
        total = total * scale
        fin[k, c] = total[0:RW].astype(jnp.bfloat16)
        for e in range(1, C):
            weight_all(k, e, c).start()
        gb[:, cols(k)] = total[RW:RW + 1]

    def weight_out(k):
        for e in range(1, C):
            weight_all(k, e, lax.rem(c - e + C, C)).wait_recv()
        gw[:, cols(k)] = fin[k].astype(jnp.float32).reshape(F, w)

    first = R - 2
    stages = [forward, chip_send, activate, backward, back_sum, finish, weight_sum, weight_total, weight_out]

    @pl.loop(0, NCH + first + len(stages) - 1)
    def _(i):
        @pl.when(i + 1 < NCH)
        def _():
            send_own(i + 1)

        for m in range(R - 1):
            @pl.when((i - m >= 0) & (i - m < NCH))
            def _():
                relay(i - m, m)

        for order, stage in reversed(list(enumerate(stages))):
            at = i - first - order

            @pl.when((at >= 0) & (at < NCH))
            def _():
                stage(at)

    gin[...] = gacc[...].astype(jnp.bfloat16)

    @pl.loop(0, NCH)
    def _(k):
        for m in range(R - 1):
            @pl.when((z - m >= 0) & (z + 1 < R))
            def _():
                z_right(k, m, z).wait_send()

            @pl.when((z + m < R) & (z >= 1))
            def _():
                z_left(k, m, z).wait_send()
        core_sum(k).wait_send()
        for d in range(1, Q):
            chip_sum(k, d).wait_send()
            slope_chip(k, d, c).wait_send()
        for d in range(Q):
            slope_core(k, d, c).wait_send()
        for j in range(R - 1):
            @pl.when(z < R - 1 - j)
            def _():
                back_right(k, R - 1 - j).wait_send()

            @pl.when(z > j)
            def _():
                back_left(k, j).wait_send()
        for e in range(1, C):
            weight_part(k, e, 0, c).wait_send()
            weight_all(k, e, c).wait_send()
        for e in range(1, R):
            weight_z(k, e, z).wait_send()


def on_device(R, C, features, cotangent, weights, bias_term, adjacency, tile_rows, tile_cols, tile_count):
    tile = adjacency.shape[-1]
    cap = adjacency.shape[2]
    B, F = features.shape
    K = B // tile
    Q = C // 2
    w = F // NCH
    RW = F // C
    pairs = C * K * R * K
    slots = jnp.arange(cap, dtype=jnp.int32)
    pair = tile_rows.reshape(cap) * (R * K) + tile_cols.reshape(cap)
    pair = jnp.where(slots < tile_count.reshape(()), pair, -1)
    hit = jnp.arange(pairs, dtype=jnp.int32)[:, None] == pair[None, :]
    inv = cap + jnp.sum(jnp.where(hit, slots[None, :] - cap, 0), axis=1, dtype=jnp.int32)
    bf, f32 = jnp.bfloat16, jnp.float32
    vmem = pl.BlockSpec(memory_space=pltpu.VMEM)
    V = pltpu.VMEM

    def sems(n):
        return pltpu.SemaphoreType.DMA((NCH, n))

    act, gin, gw, gb = pl.pallas_call(
        functools.partial(kernel, R, C, tile, cap, 1.0 / math.sqrt(B * R * C)),
        out_shape=(
            jax.ShapeDtypeStruct((B, F), bf),
            jax.ShapeDtypeStruct((B, F), bf),
            jax.ShapeDtypeStruct((F, F), f32),
            jax.ShapeDtypeStruct((1, F), f32),
        ),
        in_specs=[vmem] * 4 + [pl.BlockSpec(memory_space=pltpu.SMEM), pl.BlockSpec(memory_space=pl.ANY)],
        out_specs=(vmem,) * 4,
        scratch_shapes=[
            V((cap + 1, tile, tile), bf),
            V((C * B, R * B), bf),
            V((NCH, R, B, w), bf),
            V((NCH, Q, B, w), bf),
            V((NCH, Q, B, w), bf),
            V((NCH, Q, B, w), f32),
            V((NCH, Q, B, w), bf),
            V((NCH, Q, B, w), bf),
            V((NCH, C, w, B), bf),
            V((NCH, R, w, B), f32),
            V((NCH, R, w, B), bf),
            V((NCH, R, w, B), bf),
            V((NCH, R, w, B), bf),
            V((NCH, R, w, B), bf),
            V((F, B), bf),
            V((NCH, 1, w), f32),
            V((B, F), f32),
            V((NCH, C, RW + 16, w), bf),
            V((NCH, C, RW + 16, w), bf),
            V((NCH, R, RW + 16, w), bf),
            V((NCH, C, RW, w), bf),
            pltpu.SemaphoreType.DMA,
            sems(R), sems(R), sems(R), sems(R),
            pltpu.SemaphoreType.DMA((NCH,)), pltpu.SemaphoreType.DMA((NCH,)),
            sems(Q), sems(Q), sems(Q), sems(Q), sems(Q), sems(Q),
            sems(R), sems(R), sems(R), sems(R),
            sems(C), sems(C), sems(R), sems(R), sems(C), sems(C),
        ],
        compiler_params=pltpu.CompilerParams(
            collective_id=0, has_side_effects=True, vmem_limit_bytes=60 * 1024 * 1024
        ),
    )(features, cotangent, weights, bias_term[None, :], inv, adjacency.reshape(cap, tile, tile))
    return act, gin, gw, gb.reshape(F)


def solution(mesh):
    return jax.shard_map(
        functools.partial(on_device, mesh.shape["row"], mesh.shape["col"]),
        mesh=mesh,
        in_specs=(
            P(("row", "col"), None),
            P(("row", "col"), None),
            P(),
            P(),
            P("row", "col", None, None, None),
            P("row", "col", None),
            P("row", "col", None),
            P("row", "col"),
        ),
        out_specs=(P(("row", "col"), None), P(("row", "col"), None), P(), P()),
        check_vma=False,
    )
```

```python
import functools
import math

import jax
import jax.numpy as jnp
from jax import lax
from jax.experimental import pallas as pl
from jax.experimental.pallas import tpu as pltpu
from jax.sharding import PartitionSpec as P

MESH = pl.DeviceIdType.MESH
NCH = 4


def kernel(
    R, C, tile, cap, scale,
    feat, cot, w_ref, bias, inv, adj_hbm,
    act, gin, gw, gb,
    adj_v, A, proj, s1, r1, p1, s2, r2, ST, pc, sbR, sbL, rsR, rsL, XT, bp, gacc,
    wsend, wrecv, zsum, fin,
    adj_sem, zrs, zrr, zls, zlr, c1s, c1r, c2s, c2r, ags, agr, ocs, ocr,
    rrs, rrr, rls, rlr, wss, wsr, zss, zsr, fns, fnr,
):
    B, F = feat.shape
    w = F // NCH
    Q = C // 2
    RW = F // C
    K = B // tile
    z = lax.axis_index("row")
    c = lax.axis_index("col")
    core = lax.rem(c, 2)
    q = c // 2
    partner = (z, q * 2 + 1 - core)

    def at_q(d):
        return (z, lax.rem(q + d, Q) * 2 + core)

    def at_c(e):
        return (z, lax.rem(c + e, C))

    def at_z(e):
        return (lax.rem(z + e, R), c)

    adj_copy = pltpu.make_async_copy(adj_hbm, adj_v.at[pl.ds(0, cap)], adj_sem)
    adj_copy.start()

    barrier = pltpu.get_barrier_semaphore()
    for e in range(1, C):
        pl.semaphore_signal(barrier, inc=1, device_id=at_c(e), device_id_type=MESH)
    for e in range(1, R):
        pl.semaphore_signal(barrier, inc=1, device_id=at_z(e), device_id_type=MESH)

    def rcopy(src, dst, ss, rs, dev):
        return pltpu.make_async_remote_copy(
            src_ref=src, dst_ref=dst, send_sem=ss, recv_sem=rs, device_id=dev, device_id_type=MESH
        )

    def z_right(k, m, slot):
        return rcopy(proj.at[k, slot], proj.at[k, slot], zrs.at[k, m], zrr.at[k, m], (lax.rem(z + 1, R), c))

    def z_left(k, m, slot):
        return rcopy(proj.at[k, slot], proj.at[k, slot], zls.at[k, m], zlr.at[k, m], (lax.rem(z + R - 1, R), c))

    def core_sum(k):
        return rcopy(s1.at[k], r1.at[k], c1s.at[k], c1r.at[k], partner)

    def chip_sum(k, d):
        return rcopy(s2.at[k, d], r2.at[k, d], c2s.at[k, d], c2r.at[k, d], at_q(d))

    def slope_chip(k, d, slot):
        return rcopy(ST.at[k, slot], ST.at[k, slot], ags.at[k, d], agr.at[k, d], at_q(d))

    def slope_core(k, d, slot):
        return rcopy(ST.at[k, slot], ST.at[k, slot], ocs.at[k, d], ocr.at[k, d], partner)

    def back_right(k, t):
        return rcopy(sbR.at[k, t], rsR.at[k, t], rrs.at[k, t], rrr.at[k, t], (lax.rem(z + 1, R), c))

    def back_left(k, t):
        return rcopy(sbL.at[k, t], rsL.at[k, t], rls.at[k, t], rlr.at[k, t], (lax.rem(z + R - 1, R), c))

    def weight_part(k, e, src, slot):
        return rcopy(wsend.at[k, src], wrecv.at[k, slot], wss.at[k, e], wsr.at[k, e], at_c(e))

    def weight_z(k, e, slot):
        return rcopy(zsum.at[k, slot], zsum.at[k, slot], zss.at[k, e], zsr.at[k, e], at_z(e))

    def weight_all(k, e, slot):
        return rcopy(fin.at[k, slot], fin.at[k, slot], fns.at[k, e], fnr.at[k, e], at_c(e))

    def cols(k):
        return pl.ds(pl.multiple_of(k * w, w), w)

    full = jnp.dot(feat[...], w_ref[...], preferred_element_type=jnp.float32).astype(jnp.bfloat16)
    for k in range(NCH):
        proj[k, z] = full[:, k * w:(k + 1) * w]
    pl.semaphore_wait(barrier, C + R - 2)

    def send_own(k):
        @pl.when(z + 1 < R)
        def _():
            z_right(k, 0, z).start()

        @pl.when(z >= 1)
        def _():
            z_left(k, 0, z).start()

    send_own(0)
    XT[...] = feat[...].astype(jnp.float32).T.astype(jnp.bfloat16)
    gacc[...] = jnp.zeros_like(gacc)
    adj_v[cap] = jnp.zeros((tile, tile), jnp.bfloat16)
    adj_copy.wait()

    @pl.loop(0, C * K)
    def _(rb):
        for cb in range(R * K):
            A[pl.ds(pl.multiple_of(rb * tile, tile), tile), cb * tile:(cb + 1) * tile] = adj_v[
                inv[rb * (R * K) + cb]
            ]

    def relay(k, m):
        @pl.when(z - 1 - m >= 0)
        def _():
            slot = lax.rem(z - 1 - m + R, R)
            z_right(k, m, slot).wait_recv()
            if m + 1 < R - 1:
                @pl.when(z + 1 < R)
                def _():
                    z_right(k, m + 1, slot).start()

        @pl.when(z + 1 + m < R)
        def _():
            slot = lax.rem(z + 1 + m, R)
            z_left(k, m, slot).wait_recv()
            if m + 1 < R - 1:
                @pl.when(z >= 1)
                def _():
                    z_left(k, m + 1, slot).start()

    def forward(k):
        source = proj[k].reshape(R * B, w)

        def rows_of(c2):
            return A[pl.ds(pl.multiple_of(c2 * B, B), B), :]

        @pl.loop(0, Q)
        def _(j):
            s1[k, j] = jnp.dot(
                rows_of(2 * j + 1 - core), source, preferred_element_type=jnp.float32
            ).astype(jnp.bfloat16)

        core_sum(k).start()

        @pl.loop(0, Q)
        def _(j):
            p1[k, j] = jnp.dot(rows_of(2 * j + core), source, preferred_element_type=jnp.float32)

    def chip_send(k):
        core_sum(k).wait_recv()
        for d in range(1, Q):
            j = lax.rem(q + d, Q)
            s2[k, d] = (p1[k, j] + r1[k, j].astype(jnp.float32)).astype(jnp.bfloat16)
            chip_sum(k, d).start()

    def activate(k):
        total = p1[k, q] + r1[k, q].astype(jnp.float32)
        for d in range(1, Q):
            chip_sum(k, d).wait_recv()
            total = total + r2[k, d].astype(jnp.float32)
        shifted = total + bias[:, cols(k)]
        sig = jax.nn.sigmoid(shifted)
        slope = cot[:, cols(k)].astype(jnp.float32) * sig * (1.0 + shifted * (1.0 - sig))
        slope = slope.astype(jnp.bfloat16).astype(jnp.float32)
        ST[k, c] = slope.T.astype(jnp.bfloat16)
        for d in range(1, Q):
            slope_chip(k, d, c).start()
        slope_core(k, 0, c).start()
        act[:, cols(k)] = (shifted * sig).astype(jnp.bfloat16)
        bp[k] = jnp.sum(slope, axis=0, keepdims=True)

    def backward(k):
        for d in range(1, Q):
            slot = lax.rem(q - d + Q, Q) * 2 + core
            slope_chip(k, d, slot).wait_recv()
            slope_core(k, d, slot).start()
        for d in range(Q):
            slot = lax.rem(q - d + Q, Q) * 2 + 1 - core
            slope_core(k, d, slot).wait_recv()

        @pl.loop(0, R)
        def _(t):
            acc = jnp.zeros((w, B), jnp.float32)
            for j in range(C):
                acc = acc + jnp.dot(
                    ST[k, j],
                    A[j * B:(j + 1) * B, pl.ds(pl.multiple_of(t * B, B), B)],
                    preferred_element_type=jnp.float32,
                )
            pc[k, t] = acc

    def back_hop(j):
        def hop(k):
            @pl.when(z == j)
            def _():
                for t in range(R - 1, j - 1, -1):
                    if j >= 1:
                        back_right(k, t).wait_recv()
                    if t > j:
                        total = pc[k, t]
                        if j >= 1:
                            total = total + rsR[k, t].astype(jnp.float32)
                        sbR[k, t] = total.astype(jnp.bfloat16)
                        back_right(k, t).start()

            me = R - 1 - j

            @pl.when(z == me)
            def _():
                for t in range(0, me + 1):
                    if me < R - 1:
                        back_left(k, t).wait_recv()
                    if t < me:
                        total = pc[k, t]
                        if me < R - 1:
                            total = total + rsL[k, t].astype(jnp.float32)
                        sbL[k, t] = total.astype(jnp.bfloat16)
                        back_left(k, t).start()

        return hop

    def finish(k):
        @pl.when(z >= 1)
        def _():
            pc[k, z] = pc[k, z] + rsR[k, z].astype(jnp.float32)

        @pl.when(z < R - 1)
        def _():
            pc[k, z] = pc[k, z] + rsL[k, z].astype(jnp.float32)

        back = pc[k, z].T.astype(jnp.bfloat16)
        part = jnp.dot(XT[...], back, preferred_element_type=jnp.float32)
        wsend[k, :, 0:RW, :] = part.astype(jnp.bfloat16).reshape(C, RW, w)
        wsend[k, :, RW:RW + 16, :] = jnp.broadcast_to(bp[k].astype(jnp.bfloat16)[None], (C, 16, w))
        for e in range(1, C):
            weight_part(k, e, lax.rem(c + e, C), c).start()
        wrecv[k, c] = wsend[k, c]
        gacc[...] += lax.dot_general(
            back, w_ref[:, cols(k)], (((1,), (1,)), ((), ())), preferred_element_type=jnp.float32
        )

    def weight_sum(k):
        for e in range(1, C):
            weight_part(k, e, 0, lax.rem(c - e + C, C)).wait_recv()
        total = wrecv[k, 0].astype(jnp.float32)
        for j in range(1, C):
            total = total + wrecv[k, j].astype(jnp.float32)
        zsum[k, z] = total.astype(jnp.bfloat16)
        for e in range(1, R):
            weight_z(k, e, z).start()

    def weight_total(k):
        for e in range(1, R):
            weight_z(k, e, lax.rem(z - e + R, R)).wait_recv()
        total = zsum[k, 0].astype(jnp.float32)
        for j in range(1, R):
            total = total + zsum[k, j].astype(jnp.float32)
        total = total * scale
        fin[k, c] = total[0:RW].astype(jnp.bfloat16)
        for e in range(1, C):
            weight_all(k, e, c).start()
        gb[:, cols(k)] = total[RW:RW + 1]

    def weight_out(k):
        for e in range(1, C):
            weight_all(k, e, lax.rem(c - e + C, C)).wait_recv()
        gw[:, cols(k)] = fin[k].astype(jnp.float32).reshape(F, w)

    first = R - 2
    stages = [forward, chip_send, activate, backward] + [back_hop(j) for j in range(R)] + [finish, weight_sum, weight_total, weight_out]

    @pl.loop(0, NCH + first + len(stages) - 1)
    def _(i):
        @pl.when(i + 1 < NCH)
        def _():
            send_own(i + 1)

        for m in range(R - 1):
            @pl.when((i - m >= 0) & (i - m < NCH))
            def _():
                relay(i - m, m)

        for order, stage in reversed(list(enumerate(stages))):
            at = i - first - order

            @pl.when((at >= 0) & (at < NCH))
            def _():
                stage(at)

    gin[...] = gacc[...].astype(jnp.bfloat16)

    @pl.loop(0, NCH)
    def _(k):
        for m in range(R - 1):
            @pl.when((z - m >= 0) & (z + 1 < R))
            def _():
                z_right(k, m, z).wait_send()

            @pl.when((z + m < R) & (z >= 1))
            def _():
                z_left(k, m, z).wait_send()
        core_sum(k).wait_send()
        for d in range(1, Q):
            chip_sum(k, d).wait_send()
            slope_chip(k, d, c).wait_send()
        for d in range(Q):
            slope_core(k, d, c).wait_send()
        for j in range(R - 1):
            @pl.when(z < R - 1 - j)
            def _():
                back_right(k, R - 1 - j).wait_send()

            @pl.when(z > j)
            def _():
                back_left(k, j).wait_send()
        for e in range(1, C):
            weight_part(k, e, 0, c).wait_send()
            weight_all(k, e, c).wait_send()
        for e in range(1, R):
            weight_z(k, e, z).wait_send()


def on_device(R, C, features, cotangent, weights, bias_term, adjacency, tile_rows, tile_cols, tile_count):
    tile = adjacency.shape[-1]
    cap = adjacency.shape[2]
    B, F = features.shape
    K = B // tile
    Q = C // 2
    w = F // NCH
    RW = F // C
    pairs = C * K * R * K
    slots = jnp.arange(cap, dtype=jnp.int32)
    pair = tile_rows.reshape(cap) * (R * K) + tile_cols.reshape(cap)
    pair = jnp.where(slots < tile_count.reshape(()), pair, -1)
    hit = jnp.arange(pairs, dtype=jnp.int32)[:, None] == pair[None, :]
    inv = cap + jnp.sum(jnp.where(hit, slots[None, :] - cap, 0), axis=1, dtype=jnp.int32)
    bf, f32 = jnp.bfloat16, jnp.float32
    vmem = pl.BlockSpec(memory_space=pltpu.VMEM)
    V = pltpu.VMEM

    def sems(n):
        return pltpu.SemaphoreType.DMA((NCH, n))

    act, gin, gw, gb = pl.pallas_call(
        functools.partial(kernel, R, C, tile, cap, 1.0 / math.sqrt(B * R * C)),
        out_shape=(
            jax.ShapeDtypeStruct((B, F), bf),
            jax.ShapeDtypeStruct((B, F), bf),
            jax.ShapeDtypeStruct((F, F), f32),
            jax.ShapeDtypeStruct((1, F), f32),
        ),
        in_specs=[vmem] * 4 + [pl.BlockSpec(memory_space=pltpu.SMEM), pl.BlockSpec(memory_space=pl.ANY)],
        out_specs=(vmem,) * 4,
        scratch_shapes=[
            V((cap + 1, tile, tile), bf),
            V((C * B, R * B), bf),
            V((NCH, R, B, w), bf),
            V((NCH, Q, B, w), bf),
            V((NCH, Q, B, w), bf),
            V((NCH, Q, B, w), f32),
            V((NCH, Q, B, w), bf),
            V((NCH, Q, B, w), bf),
            V((NCH, C, w, B), bf),
            V((NCH, R, w, B), f32),
            V((NCH, R, w, B), bf),
            V((NCH, R, w, B), bf),
            V((NCH, R, w, B), bf),
            V((NCH, R, w, B), bf),
            V((F, B), bf),
            V((NCH, 1, w), f32),
            V((B, F), f32),
            V((NCH, C, RW + 16, w), bf),
            V((NCH, C, RW + 16, w), bf),
            V((NCH, R, RW + 16, w), bf),
            V((NCH, C, RW, w), bf),
            pltpu.SemaphoreType.DMA,
            sems(R), sems(R), sems(R), sems(R),
            pltpu.SemaphoreType.DMA((NCH,)), pltpu.SemaphoreType.DMA((NCH,)),
            sems(Q), sems(Q), sems(Q), sems(Q), sems(Q), sems(Q),
            sems(R), sems(R), sems(R), sems(R),
            sems(C), sems(C), sems(R), sems(R), sems(C), sems(C),
        ],
        compiler_params=pltpu.CompilerParams(
            collective_id=0, has_side_effects=True, vmem_limit_bytes=60 * 1024 * 1024
        ),
    )(features, cotangent, weights, bias_term[None, :], inv, adjacency.reshape(cap, tile, tile))
    return act, gin, gw, gb.reshape(F)


def solution(mesh):
    return jax.shard_map(
        functools.partial(on_device, mesh.shape["row"], mesh.shape["col"]),
        mesh=mesh,
        in_specs=(
            P(("row", "col"), None),
            P(("row", "col"), None),
            P(),
            P(),
            P("row", "col", None, None, None),
            P("row", "col", None),
            P("row", "col", None),
            P("row", "col"),
        ),
        out_specs=(P(("row", "col"), None), P(("row", "col"), None), P(), P()),
        check_vma=False,
    )
```

```python
import functools
import math

import jax
import jax.numpy as jnp
from jax import lax
from jax.experimental import pallas as pl
from jax.experimental.pallas import tpu as pltpu
from jax.sharding import PartitionSpec as P

MESH = pl.DeviceIdType.MESH
NCH = 2


def kernel(
    R, C, tile, cap, scale,
    feat, cot, w_ref, bias, inv, adj_hbm,
    act, gin, gw, gb,
    adj_v, A, proj, s1, r1, p1, s2, r2, ST, pc, sbR, sbL, rsR, rsL, XT, bp, gacc,
    wsend, wrecv, zsum, fin,
    adj_sem, zrs, zrr, zls, zlr, c1s, c1r, c2s, c2r, ags, agr, ocs, ocr,
    rrs, rrr, rls, rlr, wss, wsr, zss, zsr, fns, fnr,
):
    B, F = feat.shape
    w = F // NCH
    Q = C // 2
    RW = F // C
    K = B // tile
    z = lax.axis_index("row")
    c = lax.axis_index("col")
    core = lax.rem(c, 2)
    q = c // 2
    partner = (z, q * 2 + 1 - core)

    def at_q(d):
        return (z, lax.rem(q + d, Q) * 2 + core)

    def at_c(e):
        return (z, lax.rem(c + e, C))

    def at_z(e):
        return (lax.rem(z + e, R), c)

    adj_copy = pltpu.make_async_copy(adj_hbm, adj_v.at[pl.ds(0, cap)], adj_sem)
    adj_copy.start()

    barrier = pltpu.get_barrier_semaphore()
    for e in range(1, C):
        pl.semaphore_signal(barrier, inc=1, device_id=at_c(e), device_id_type=MESH)
    for e in range(1, R):
        pl.semaphore_signal(barrier, inc=1, device_id=at_z(e), device_id_type=MESH)

    def rcopy(src, dst, ss, rs, dev):
        return pltpu.make_async_remote_copy(
            src_ref=src, dst_ref=dst, send_sem=ss, recv_sem=rs, device_id=dev, device_id_type=MESH
        )

    def z_right(k, m, slot):
        return rcopy(proj.at[k, slot], proj.at[k, slot], zrs.at[k, m], zrr.at[k, m], (lax.rem(z + 1, R), c))

    def z_left(k, m, slot):
        return rcopy(proj.at[k, slot], proj.at[k, slot], zls.at[k, m], zlr.at[k, m], (lax.rem(z + R - 1, R), c))

    def core_sum(k):
        return rcopy(s1.at[k], r1.at[k], c1s.at[k], c1r.at[k], partner)

    def chip_sum(k, d):
        return rcopy(s2.at[k, d], r2.at[k, d], c2s.at[k], c2r.at[k], at_q(d))

    def slope_chip(k, d, slot):
        return rcopy(ST.at[k, slot], ST.at[k, slot], ags.at[k, d], agr.at[k, d], at_q(d))

    def slope_core(k, slot):
        return rcopy(ST.at[k, slot], ST.at[k, slot], ocs.at[k], ocr.at[k], partner)

    def back_right(k, t):
        return rcopy(sbR.at[k, t], rsR.at[k, t], rrs.at[k, t], rrr.at[k, t], (lax.rem(z + 1, R), c))

    def back_left(k, t):
        return rcopy(sbL.at[k, t], rsL.at[k, t], rls.at[k, t], rlr.at[k, t], (lax.rem(z + R - 1, R), c))

    def weight_part(k, e, src, slot):
        return rcopy(wsend.at[k, src], wrecv.at[k, slot], wss.at[k], wsr.at[k], at_c(e))

    def weight_z(k, e, slot):
        return rcopy(zsum.at[k, slot], zsum.at[k, slot], zss.at[k], zsr.at[k], at_z(e))

    def weight_all(k, e, slot):
        return rcopy(fin.at[k, slot], fin.at[k, slot], fns.at[k], fnr.at[k], at_c(e))

    def chip_sum_all(k):
        return rcopy(s2.at[k, pl.ds(0, Q - 1)], r2.at[k, pl.ds(0, Q - 1)], c2s.at[k], c2r.at[k], partner)

    def slope_core_all(k):
        return rcopy(ST.at[k, pl.ds(0, Q)], ST.at[k, pl.ds(0, Q)], ocs.at[k], ocr.at[k], partner)

    def weight_part_group(k):
        return rcopy(wsend.at[k, pl.ds(0, C - 1)], wrecv.at[k, pl.ds(0, C - 1)], wss.at[k], wsr.at[k], partner)

    def weight_z_group(k):
        return rcopy(zsum.at[k, pl.ds(0, R - 1)], zsum.at[k, pl.ds(0, R - 1)], zss.at[k], zsr.at[k], partner)

    def weight_all_group(k):
        return rcopy(fin.at[k, pl.ds(0, C - 1)], fin.at[k, pl.ds(0, C - 1)], fns.at[k], fnr.at[k], partner)

    def cols(k):
        return pl.ds(pl.multiple_of(k * w, w), w)

    full = jnp.dot(feat[...], w_ref[...], preferred_element_type=jnp.float32).astype(jnp.bfloat16)
    for k in range(NCH):
        proj[k, z] = full[:, k * w:(k + 1) * w]
    pl.semaphore_wait(barrier, C + R - 2)

    def send_own(k):
        @pl.when(z + 1 < R)
        def _():
            z_right(k, 0, z).start()

        @pl.when(z >= 1)
        def _():
            z_left(k, 0, z).start()

    send_own(0)
    XT[...] = feat[...].astype(jnp.float32).T.astype(jnp.bfloat16)
    gacc[...] = jnp.zeros_like(gacc)
    adj_v[cap] = jnp.zeros((tile, tile), jnp.bfloat16)
    adj_copy.wait()

    @pl.loop(0, C * K)
    def _(rb):
        for cb in range(R * K):
            A[pl.ds(pl.multiple_of(rb * tile, tile), tile), cb * tile:(cb + 1) * tile] = adj_v[
                inv[rb * (R * K) + cb]
            ]

    def relay(k, m):
        @pl.when(z - 1 - m >= 0)
        def _():
            slot = lax.rem(z - 1 - m + R, R)
            z_right(k, m, slot).wait_recv()
            if m + 1 < R - 1:
                @pl.when(z + 1 < R)
                def _():
                    z_right(k, m + 1, slot).start()

        @pl.when(z + 1 + m < R)
        def _():
            slot = lax.rem(z + 1 + m, R)
            z_left(k, m, slot).wait_recv()
            if m + 1 < R - 1:
                @pl.when(z >= 1)
                def _():
                    z_left(k, m + 1, slot).start()

    def forward(k):
        source = proj[k].reshape(R * B, w)

        def rows_of(c2):
            return A[pl.ds(pl.multiple_of(c2 * B, B), B), :]

        @pl.loop(0, Q)
        def _(j):
            s1[k, j] = jnp.dot(
                rows_of(2 * j + 1 - core), source, preferred_element_type=jnp.float32
            ).astype(jnp.bfloat16)

        core_sum(k).start()

        @pl.loop(0, Q)
        def _(j):
            p1[k, j] = jnp.dot(rows_of(2 * j + core), source, preferred_element_type=jnp.float32)

    def chip_send(k):
        core_sum(k).wait_recv()
        for d in range(1, Q):
            j = lax.rem(q + d, Q)
            s2[k, d] = (p1[k, j] + r1[k, j].astype(jnp.float32)).astype(jnp.bfloat16)
            chip_sum(k, d).start()

    def activate(k):
        total = p1[k, q] + r1[k, q].astype(jnp.float32)
        chip_sum_all(k).wait_recv()
        for d in range(1, Q):
            total = total + r2[k, d].astype(jnp.float32)
        shifted = total + bias[:, cols(k)]
        sig = jax.nn.sigmoid(shifted)
        slope = cot[:, cols(k)].astype(jnp.float32) * sig * (1.0 + shifted * (1.0 - sig))
        slope = slope.astype(jnp.bfloat16).astype(jnp.float32)
        ST[k, c] = slope.T.astype(jnp.bfloat16)
        for d in range(1, Q):
            slope_chip(k, d, c).start()
        slope_core(k, c).start()
        act[:, cols(k)] = (shifted * sig).astype(jnp.bfloat16)
        bp[k] = jnp.sum(slope, axis=0, keepdims=True)

    def backward(k):
        for d in range(1, Q):
            slot = lax.rem(q - d + Q, Q) * 2 + core
            slope_chip(k, d, slot).wait_recv()
            slope_core(k, slot).start()
        slope_core_all(k).wait_recv()

        @pl.loop(0, R)
        def _(t):
            acc = jnp.zeros((w, B), jnp.float32)
            for j in range(C):
                acc = acc + jnp.dot(
                    ST[k, j],
                    A[j * B:(j + 1) * B, pl.ds(pl.multiple_of(t * B, B), B)],
                    preferred_element_type=jnp.float32,
                )
            pc[k, t] = acc

    def back_hop(j):
        def hop(k):
            @pl.when(z == j)
            def _():
                for t in range(R - 1, j - 1, -1):
                    if j >= 1:
                        back_right(k, t).wait_recv()
                    if t > j:
                        total = pc[k, t]
                        if j >= 1:
                            total = total + rsR[k, t].astype(jnp.float32)
                        sbR[k, t] = total.astype(jnp.bfloat16)
                        back_right(k, t).start()

            me = R - 1 - j

            @pl.when(z == me)
            def _():
                for t in range(0, me + 1):
                    if me < R - 1:
                        back_left(k, t).wait_recv()
                    if t < me:
                        total = pc[k, t]
                        if me < R - 1:
                            total = total + rsL[k, t].astype(jnp.float32)
                        sbL[k, t] = total.astype(jnp.bfloat16)
                        back_left(k, t).start()

        return hop

    def finish(k):
        @pl.when(z >= 1)
        def _():
            pc[k, z] = pc[k, z] + rsR[k, z].astype(jnp.float32)

        @pl.when(z < R - 1)
        def _():
            pc[k, z] = pc[k, z] + rsL[k, z].astype(jnp.float32)

        back = pc[k, z].T.astype(jnp.bfloat16)
        part = jnp.dot(XT[...], back, preferred_element_type=jnp.float32)
        wsend[k, :, 0:RW, :] = part.astype(jnp.bfloat16).reshape(C, RW, w)
        wsend[k, :, RW:RW + 16, :] = jnp.broadcast_to(bp[k].astype(jnp.bfloat16)[None], (C, 16, w))
        for e in range(1, C):
            weight_part(k, e, lax.rem(c + e, C), c).start()
        wrecv[k, c] = wsend[k, c]
        gacc[...] += lax.dot_general(
            back, w_ref[:, cols(k)], (((1,), (1,)), ((), ())), preferred_element_type=jnp.float32
        )

        @pl.when(k == NCH - 1)
        def _():
            gin[...] = gacc[...].astype(jnp.bfloat16)

    def weight_sum(k):
        weight_part_group(k).wait_recv()
        total = wrecv[k, 0].astype(jnp.float32)
        for j in range(1, C):
            total = total + wrecv[k, j].astype(jnp.float32)
        zsum[k, z] = total.astype(jnp.bfloat16)
        for e in range(1, R):
            weight_z(k, e, z).start()

    def weight_total(k):
        weight_z_group(k).wait_recv()
        total = zsum[k, 0].astype(jnp.float32)
        for j in range(1, R):
            total = total + zsum[k, j].astype(jnp.float32)
        total = total * scale
        fin[k, c] = total[0:RW].astype(jnp.bfloat16)
        for e in range(1, C):
            weight_all(k, e, c).start()
        gb[:, cols(k)] = total[RW:RW + 1]

    def weight_out(k):
        weight_all_group(k).wait_recv()
        gw[:, cols(k)] = fin[k].reshape(F, w)

    first = R - 2
    stages = [forward, chip_send, activate, backward] + [back_hop(j) for j in range(R)] + [finish, weight_sum, weight_total, weight_out]

    @pl.loop(0, NCH + first + len(stages) - 1)
    def _(i):
        @pl.when(i + 1 < NCH)
        def _():
            send_own(i + 1)

        for m in range(R - 1):
            @pl.when((i - m >= 0) & (i - m < NCH))
            def _():
                relay(i - m, m)

        for order, stage in reversed(list(enumerate(stages))):
            at = i - first - order

            @pl.when((at >= 0) & (at < NCH))
            def _():
                stage(at)

    @pl.loop(0, NCH)
    def _(k):
        for m in range(R - 1):
            @pl.when((z - m >= 0) & (z + 1 < R))
            def _():
                z_right(k, m, z).wait_send()

            @pl.when((z + m < R) & (z >= 1))
            def _():
                z_left(k, m, z).wait_send()
        core_sum(k).wait_send()
        chip_sum_all(k).wait_send()
        for d in range(1, Q):
            slope_chip(k, d, c).wait_send()
        slope_core_all(k).wait_send()
        for j in range(R - 1):
            @pl.when(z < R - 1 - j)
            def _():
                back_right(k, R - 1 - j).wait_send()

            @pl.when(z > j)
            def _():
                back_left(k, j).wait_send()
        weight_part_group(k).wait_send()
        weight_z_group(k).wait_send()
        weight_all_group(k).wait_send()


def on_device(R, C, features, cotangent, weights, bias_term, adjacency, tile_rows, tile_cols, tile_count):
    tile = adjacency.shape[-1]
    cap = adjacency.shape[2]
    B, F = features.shape
    K = B // tile
    Q = C // 2
    w = F // NCH
    RW = F // C
    pairs = C * K * R * K
    slots = jnp.arange(cap, dtype=jnp.int32)
    pair = tile_rows.reshape(cap) * (R * K) + tile_cols.reshape(cap)
    pair = jnp.where(slots < tile_count.reshape(()), pair, -1)
    hit = jnp.arange(pairs, dtype=jnp.int32)[:, None] == pair[None, :]
    inv = cap + jnp.sum(jnp.where(hit, slots[None, :] - cap, 0), axis=1, dtype=jnp.int32)
    bf, f32 = jnp.bfloat16, jnp.float32
    vmem = pl.BlockSpec(memory_space=pltpu.VMEM)
    V = pltpu.VMEM

    group = pltpu.SemaphoreType.DMA((NCH,))

    def sems(n):
        return pltpu.SemaphoreType.DMA((NCH, n))

    act, gin, gw, gb = pl.pallas_call(
        functools.partial(kernel, R, C, tile, cap, 1.0 / math.sqrt(B * R * C)),
        out_shape=(
            jax.ShapeDtypeStruct((B, F), bf),
            jax.ShapeDtypeStruct((B, F), bf),
            jax.ShapeDtypeStruct((F, F), bf),
            jax.ShapeDtypeStruct((1, F), f32),
        ),
        in_specs=[vmem] * 4 + [pl.BlockSpec(memory_space=pltpu.SMEM), pl.BlockSpec(memory_space=pl.ANY)],
        out_specs=(vmem,) * 4,
        scratch_shapes=[
            V((cap + 1, tile, tile), bf),
            V((C * B, R * B), bf),
            V((NCH, R, B, w), bf),
            V((NCH, Q, B, w), bf),
            V((NCH, Q, B, w), bf),
            V((NCH, Q, B, w), f32),
            V((NCH, Q, B, w), bf),
            V((NCH, Q, B, w), bf),
            V((NCH, C, w, B), bf),
            V((NCH, R, w, B), f32),
            V((NCH, R, w, B), bf),
            V((NCH, R, w, B), bf),
            V((NCH, R, w, B), bf),
            V((NCH, R, w, B), bf),
            V((F, B), bf),
            V((NCH, 1, w), f32),
            V((B, F), f32),
            V((NCH, C, RW + 16, w), bf),
            V((NCH, C, RW + 16, w), bf),
            V((NCH, R, RW + 16, w), bf),
            V((NCH, C, RW, w), bf),
            pltpu.SemaphoreType.DMA,
            sems(R), sems(R), sems(R), sems(R),
            group, group,
            group, group, sems(Q), sems(Q), group, group,
            sems(R), sems(R), sems(R), sems(R),
            group, group, group, group, group, group,
        ],
        compiler_params=pltpu.CompilerParams(
            collective_id=0, has_side_effects=True, vmem_limit_bytes=60 * 1024 * 1024
        ),
    )(features, cotangent, weights, bias_term[None, :], inv, adjacency.reshape(cap, tile, tile))
    return act, gin, gw.astype(f32), gb.reshape(F)


def solution(mesh):
    return jax.shard_map(
        functools.partial(on_device, mesh.shape["row"], mesh.shape["col"]),
        mesh=mesh,
        in_specs=(
            P(("row", "col"), None),
            P(("row", "col"), None),
            P(),
            P(),
            P("row", "col", None, None, None),
            P("row", "col", None),
            P("row", "col", None),
            P("row", "col"),
        ),
        out_specs=(P(("row", "col"), None), P(("row", "col"), None), P(), P()),
        check_vma=False,
    )
```

```python
import functools
import math

import jax
import jax.numpy as jnp
from jax import lax
from jax.experimental import pallas as pl
from jax.experimental.pallas import tpu as pltpu
from jax.sharding import PartitionSpec as P

MESH = pl.DeviceIdType.MESH
NCH = 4


def kernel(
    R, C, tile, cap, scale,
    feat, cot, w_ref, bias, inv, adj_hbm,
    act, gin, gw, gb,
    adj_v, A, proj, s1, r1, p1, s2, r2, ST, pc, sbR, sbL, rsR, rsL, XT, bp, gacc,
    wsend, wrecv, zsum, fin,
    adj_sem, zrs, zrr, zls, zlr, c1s, c1r, c2s, c2r, ags, agr, ocs, ocr,
    rrs, rrr, rls, rlr, wss, wsr, zss, zsr, fns, fnr,
):
    B, F = feat.shape
    w = F // NCH
    Q = C // 2
    RW = F // C
    K = B // tile
    z = lax.axis_index("row")
    c = lax.axis_index("col")
    core = lax.rem(c, 2)
    q = c // 2
    partner = (z, q * 2 + 1 - core)

    def at_q(d):
        return (z, lax.rem(q + d, Q) * 2 + core)

    def at_c(e):
        return (z, lax.rem(c + e, C))

    def at_z(e):
        return (lax.rem(z + e, R), c)

    adj_copy = pltpu.make_async_copy(adj_hbm, adj_v.at[pl.ds(0, cap)], adj_sem)
    adj_copy.start()

    barrier = pltpu.get_barrier_semaphore()
    for e in range(1, C):
        pl.semaphore_signal(barrier, inc=1, device_id=at_c(e), device_id_type=MESH)
    for e in range(1, R):
        pl.semaphore_signal(barrier, inc=1, device_id=at_z(e), device_id_type=MESH)

    def rcopy(src, dst, ss, rs, dev):
        return pltpu.make_async_remote_copy(
            src_ref=src, dst_ref=dst, send_sem=ss, recv_sem=rs, device_id=dev, device_id_type=MESH
        )

    def z_right(k, m, slot):
        return rcopy(proj.at[k, slot], proj.at[k, slot], zrs.at[k, m], zrr.at[k, m], (lax.rem(z + 1, R), c))

    def z_left(k, m, slot):
        return rcopy(proj.at[k, slot], proj.at[k, slot], zls.at[k, m], zlr.at[k, m], (lax.rem(z + R - 1, R), c))

    def core_sum(k):
        return rcopy(s1.at[k], r1.at[k], c1s.at[k], c1r.at[k], partner)

    def chip_sum(k, d):
        return rcopy(s2.at[k, d], r2.at[k, d], c2s.at[k], c2r.at[k], at_q(d))

    def slope_chip(k, d, slot):
        return rcopy(ST.at[k, slot], ST.at[k, slot], ags.at[k, d], agr.at[k, d], at_q(d))

    def slope_core(k, slot):
        return rcopy(ST.at[k, slot], ST.at[k, slot], ocs.at[k], ocr.at[k], partner)

    def back_right(k, t):
        return rcopy(sbR.at[k, t], rsR.at[k, t], rrs.at[k, t], rrr.at[k, t], (lax.rem(z + 1, R), c))

    def back_left(k, t):
        return rcopy(sbL.at[k, t], rsL.at[k, t], rls.at[k, t], rlr.at[k, t], (lax.rem(z + R - 1, R), c))

    def weight_part(k, e, src, slot):
        return rcopy(wsend.at[k, src], wrecv.at[k, slot], wss.at[k], wsr.at[k], at_c(e))

    def weight_z(k, e, slot):
        return rcopy(zsum.at[k, slot], zsum.at[k, slot], zss.at[k], zsr.at[k], at_z(e))

    def weight_all(k, e, slot):
        return rcopy(fin.at[k, slot], fin.at[k, slot], fns.at[k], fnr.at[k], at_c(e))

    def chip_sum_all(k):
        return rcopy(s2.at[k, pl.ds(0, Q - 1)], r2.at[k, pl.ds(0, Q - 1)], c2s.at[k], c2r.at[k], partner)

    def slope_core_all(k):
        return rcopy(ST.at[k, pl.ds(0, Q)], ST.at[k, pl.ds(0, Q)], ocs.at[k], ocr.at[k], partner)

    def weight_part_group(k):
        return rcopy(wsend.at[k, pl.ds(0, C - 1)], wrecv.at[k, pl.ds(0, C - 1)], wss.at[k], wsr.at[k], partner)

    def weight_z_group(k):
        return rcopy(zsum.at[k, pl.ds(0, R - 1)], zsum.at[k, pl.ds(0, R - 1)], zss.at[k], zsr.at[k], partner)

    def weight_all_group(k):
        return rcopy(fin.at[k, pl.ds(0, C - 1)], fin.at[k, pl.ds(0, C - 1)], fns.at[k], fnr.at[k], partner)

    def cols(k):
        return pl.ds(pl.multiple_of(k * w, w), w)

    full = jnp.dot(feat[...], w_ref[...], preferred_element_type=jnp.float32).astype(jnp.bfloat16)
    for k in range(NCH):
        proj[k, z] = full[:, k * w:(k + 1) * w]
    pl.semaphore_wait(barrier, C + R - 2)

    def send_own(k):
        @pl.when(z + 1 < R)
        def _():
            z_right(k, 0, z).start()

        @pl.when(z >= 1)
        def _():
            z_left(k, 0, z).start()

    send_own(0)
    XT[...] = feat[...].astype(jnp.float32).T.astype(jnp.bfloat16)
    gacc[...] = jnp.zeros_like(gacc)
    adj_v[cap] = jnp.zeros((tile, tile), jnp.bfloat16)
    adj_copy.wait()

    @pl.loop(0, C * K)
    def _(rb):
        for cb in range(R * K):
            A[pl.ds(pl.multiple_of(rb * tile, tile), tile), cb * tile:(cb + 1) * tile] = adj_v[
                inv[rb * (R * K) + cb]
            ]

    def relay(k, m):
        @pl.when(z - 1 - m >= 0)
        def _():
            slot = lax.rem(z - 1 - m + R, R)
            z_right(k, m, slot).wait_recv()
            if m + 1 < R - 1:
                @pl.when(z + 1 < R)
                def _():
                    z_right(k, m + 1, slot).start()

        @pl.when(z + 1 + m < R)
        def _():
            slot = lax.rem(z + 1 + m, R)
            z_left(k, m, slot).wait_recv()
            if m + 1 < R - 1:
                @pl.when(z >= 1)
                def _():
                    z_left(k, m + 1, slot).start()

    def forward(k):
        source = proj[k].reshape(R * B, w)

        def rows_of(c2):
            return A[pl.ds(pl.multiple_of(c2 * B, B), B), :]

        @pl.loop(0, Q)
        def _(j):
            s1[k, j] = jnp.dot(
                rows_of(2 * j + 1 - core), source, preferred_element_type=jnp.float32
            ).astype(jnp.bfloat16)

        core_sum(k).start()

        @pl.loop(0, Q)
        def _(j):
            p1[k, j] = jnp.dot(rows_of(2 * j + core), source, preferred_element_type=jnp.float32)

    def chip_send(k):
        core_sum(k).wait_recv()
        for d in range(1, Q):
            j = lax.rem(q + d, Q)
            s2[k, d] = (p1[k, j] + r1[k, j].astype(jnp.float32)).astype(jnp.bfloat16)
            chip_sum(k, d).start()

    def activate(k):
        total = p1[k, q] + r1[k, q].astype(jnp.float32)
        chip_sum_all(k).wait_recv()
        for d in range(1, Q):
            total = total + r2[k, d].astype(jnp.float32)
        shifted = total + bias[:, cols(k)]
        sig = jax.nn.sigmoid(shifted)
        slope = cot[:, cols(k)].astype(jnp.float32) * sig * (1.0 + shifted * (1.0 - sig))
        slope = slope.astype(jnp.bfloat16).astype(jnp.float32)
        ST[k, c] = slope.T.astype(jnp.bfloat16)
        for d in range(1, Q):
            slope_chip(k, d, c).start()
        slope_core(k, c).start()
        act[:, cols(k)] = (shifted * sig).astype(jnp.bfloat16)
        bp[k] = jnp.sum(slope, axis=0, keepdims=True)

    def slope_pass(k):
        for d in range(1, Q):
            slot = lax.rem(q - d + Q, Q) * 2 + core
            slope_chip(k, d, slot).wait_recv()
            slope_core(k, slot).start()

    def backward(k):
        slope_core_all(k).wait_recv()

        @pl.loop(0, R)
        def _(t):
            acc = jnp.zeros((w, B), jnp.float32)
            for j in range(C):
                acc = acc + jnp.dot(
                    ST[k, j],
                    A[j * B:(j + 1) * B, pl.ds(pl.multiple_of(t * B, B), B)],
                    preferred_element_type=jnp.float32,
                )
            pc[k, t] = acc

    def back_hop(j):
        def hop(k):
            @pl.when(z == j)
            def _():
                for t in range(R - 1, j - 1, -1):
                    if j >= 1:
                        back_right(k, t).wait_recv()
                    if t > j:
                        total = pc[k, t]
                        if j >= 1:
                            total = total + rsR[k, t].astype(jnp.float32)
                        sbR[k, t] = total.astype(jnp.bfloat16)
                        back_right(k, t).start()

            me = R - 1 - j

            @pl.when(z == me)
            def _():
                for t in range(0, me + 1):
                    if me < R - 1:
                        back_left(k, t).wait_recv()
                    if t < me:
                        total = pc[k, t]
                        if me < R - 1:
                            total = total + rsL[k, t].astype(jnp.float32)
                        sbL[k, t] = total.astype(jnp.bfloat16)
                        back_left(k, t).start()

        return hop

    def finish(k):
        @pl.when(z >= 1)
        def _():
            pc[k, z] = pc[k, z] + rsR[k, z].astype(jnp.float32)

        @pl.when(z < R - 1)
        def _():
            pc[k, z] = pc[k, z] + rsL[k, z].astype(jnp.float32)

        back = pc[k, z].T.astype(jnp.bfloat16)
        part = jnp.dot(XT[...], back, preferred_element_type=jnp.float32)
        wsend[k, :, 0:RW, :] = part.astype(jnp.bfloat16).reshape(C, RW, w)
        wsend[k, :, RW:RW + 16, :] = jnp.broadcast_to(bp[k].astype(jnp.bfloat16)[None], (C, 16, w))
        for e in range(1, C):
            weight_part(k, e, lax.rem(c + e, C), c).start()
        wrecv[k, c] = wsend[k, c]
        gacc[...] += lax.dot_general(
            back, w_ref[:, cols(k)], (((1,), (1,)), ((), ())), preferred_element_type=jnp.float32
        )

        @pl.when(k == NCH - 1)
        def _():
            gin[...] = gacc[...].astype(jnp.bfloat16)

    def weight_sum(k):
        weight_part_group(k).wait_recv()
        total = wrecv[k, 0].astype(jnp.float32)
        for j in range(1, C):
            total = total + wrecv[k, j].astype(jnp.float32)
        zsum[k, z] = total.astype(jnp.bfloat16)
        for e in range(1, R):
            weight_z(k, e, z).start()

    def weight_total(k):
        weight_z_group(k).wait_recv()
        total = zsum[k, 0].astype(jnp.float32)
        for j in range(1, R):
            total = total + zsum[k, j].astype(jnp.float32)
        total = total * scale
        fin[k, c] = total[0:RW].astype(jnp.bfloat16)
        for e in range(1, C):
            weight_all(k, e, c).start()
        gb[:, cols(k)] = total[RW:RW + 1]

    def weight_out(k):
        weight_all_group(k).wait_recv()
        gw[:, cols(k)] = fin[k].reshape(F, w)

    first = R - 2
    stages = [(3 + j, back_hop(j)) for j in range(R - 1, 0, -1)]
    stages += [
        (2 + R, finish),
        (3, slope_pass),
        (2, activate),
        (1, chip_send),
        (0, forward),
        (3, backward),
        (3, back_hop(0)),
        (5 + R, weight_out),
        (4 + R, weight_total),
        (3 + R, weight_sum),
    ]

    @pl.loop(0, NCH + first + 5 + R)
    def _(i):
        @pl.when(i + 1 < NCH)
        def _():
            send_own(i + 1)

        for m in range(R - 1):
            @pl.when((i - m >= 0) & (i - m < NCH))
            def _():
                relay(i - m, m)

        for after, stage in stages:
            at = i - first - after

            @pl.when((at >= 0) & (at < NCH))
            def _():
                stage(at)

    @pl.loop(0, NCH)
    def _(k):
        for m in range(R - 1):
            @pl.when((z - m >= 0) & (z + 1 < R))
            def _():
                z_right(k, m, z).wait_send()

            @pl.when((z + m < R) & (z >= 1))
            def _():
                z_left(k, m, z).wait_send()
        core_sum(k).wait_send()
        chip_sum_all(k).wait_send()
        for d in range(1, Q):
            slope_chip(k, d, c).wait_send()
        slope_core_all(k).wait_send()
        for j in range(R - 1):
            @pl.when(z < R - 1 - j)
            def _():
                back_right(k, R - 1 - j).wait_send()

            @pl.when(z > j)
            def _():
                back_left(k, j).wait_send()
        weight_part_group(k).wait_send()
        weight_z_group(k).wait_send()
        weight_all_group(k).wait_send()


def on_device(R, C, features, cotangent, weights, bias_term, adjacency, tile_rows, tile_cols, tile_count):
    tile = adjacency.shape[-1]
    cap = adjacency.shape[2]
    B, F = features.shape
    K = B // tile
    Q = C // 2
    w = F // NCH
    RW = F // C
    pairs = C * K * R * K
    slots = jnp.arange(cap, dtype=jnp.int32)
    pair = tile_rows.reshape(cap) * (R * K) + tile_cols.reshape(cap)
    pair = jnp.where(slots < tile_count.reshape(()), pair, -1)
    hit = jnp.arange(pairs, dtype=jnp.int32)[:, None] == pair[None, :]
    inv = cap + jnp.sum(jnp.where(hit, slots[None, :] - cap, 0), axis=1, dtype=jnp.int32)
    bf, f32 = jnp.bfloat16, jnp.float32
    vmem = pl.BlockSpec(memory_space=pltpu.VMEM)
    V = pltpu.VMEM

    group = pltpu.SemaphoreType.DMA((NCH,))

    def sems(n):
        return pltpu.SemaphoreType.DMA((NCH, n))

    act, gin, gw, gb = pl.pallas_call(
        functools.partial(kernel, R, C, tile, cap, 1.0 / math.sqrt(B * R * C)),
        out_shape=(
            jax.ShapeDtypeStruct((B, F), bf),
            jax.ShapeDtypeStruct((B, F), bf),
            jax.ShapeDtypeStruct((F, F), bf),
            jax.ShapeDtypeStruct((1, F), f32),
        ),
        in_specs=[vmem] * 4 + [pl.BlockSpec(memory_space=pltpu.SMEM), pl.BlockSpec(memory_space=pl.ANY)],
        out_specs=(vmem,) * 4,
        scratch_shapes=[
            V((cap + 1, tile, tile), bf),
            V((C * B, R * B), bf),
            V((NCH, R, B, w), bf),
            V((NCH, Q, B, w), bf),
            V((NCH, Q, B, w), bf),
            V((NCH, Q, B, w), f32),
            V((NCH, Q, B, w), bf),
            V((NCH, Q, B, w), bf),
            V((NCH, C, w, B), bf),
            V((NCH, R, w, B), f32),
            V((NCH, R, w, B), bf),
            V((NCH, R, w, B), bf),
            V((NCH, R, w, B), bf),
            V((NCH, R, w, B), bf),
            V((F, B), bf),
            V((NCH, 1, w), f32),
            V((B, F), f32),
            V((NCH, C, RW + 16, w), bf),
            V((NCH, C, RW + 16, w), bf),
            V((NCH, R, RW + 16, w), bf),
            V((NCH, C, RW, w), bf),
            pltpu.SemaphoreType.DMA,
            sems(R), sems(R), sems(R), sems(R),
            group, group,
            group, group, sems(Q), sems(Q), group, group,
            sems(R), sems(R), sems(R), sems(R),
            group, group, group, group, group, group,
        ],
        compiler_params=pltpu.CompilerParams(
            collective_id=0, has_side_effects=True, vmem_limit_bytes=60 * 1024 * 1024
        ),
    )(features, cotangent, weights, bias_term[None, :], inv, adjacency.reshape(cap, tile, tile))
    return act, gin, gw.astype(f32), gb.reshape(F)


def solution(mesh):
    return jax.shard_map(
        functools.partial(on_device, mesh.shape["row"], mesh.shape["col"]),
        mesh=mesh,
        in_specs=(
            P(("row", "col"), None),
            P(("row", "col"), None),
            P(),
            P(),
            P("row", "col", None, None, None),
            P("row", "col", None),
            P("row", "col", None),
            P("row", "col"),
        ),
        out_specs=(P(("row", "col"), None), P(("row", "col"), None), P(), P()),
        check_vma=False,
    )
```

```python
import functools
import math

import jax
import jax.numpy as jnp
from jax import lax
from jax.experimental import pallas as pl
from jax.experimental.pallas import tpu as pltpu
from jax.sharding import PartitionSpec as P

MESH = pl.DeviceIdType.MESH
NCH = 4


def kernel(
    R, C, tile, cap, scale,
    feat, cot, w_ref, bias, inv, adj_hbm,
    act, gin, gw, gb,
    adj_v, A, proj, s1, r1, p1, s2, r2, ST, pc, sb, rs, XT, bp, gacc,
    wsend, wrecv, zsum, fin,
    adj_sem, pjs, pjr, c1s, c1r, c2s, c2r, ags, agr, ocs, ocr,
    bks, bkr, wss, wsr, zss, zsr, fns, fnr,
):
    B, F = feat.shape
    w = F // NCH
    Q = C // 2
    RW = F // C
    K = B // tile
    z = lax.axis_index("row")
    c = lax.axis_index("col")
    core = lax.rem(c, 2)
    q = c // 2
    partner = (z, q * 2 + 1 - core)

    def at_q(d):
        return (z, lax.rem(q + d, Q) * 2 + core)

    def at_c(e):
        return (z, lax.rem(c + e, C))

    def at_z(e):
        return (lax.rem(z + e, R), c)

    adj_copy = pltpu.make_async_copy(adj_hbm, adj_v.at[pl.ds(0, cap)], adj_sem)
    adj_copy.start()

    barrier = pltpu.get_barrier_semaphore()
    for e in range(1, C):
        pl.semaphore_signal(barrier, inc=1, device_id=at_c(e), device_id_type=MESH)
    for e in range(1, R):
        pl.semaphore_signal(barrier, inc=1, device_id=at_z(e), device_id_type=MESH)

    def rcopy(src, dst, ss, rs, dev):
        return pltpu.make_async_remote_copy(
            src_ref=src, dst_ref=dst, send_sem=ss, recv_sem=rs, device_id=dev, device_id_type=MESH
        )

    def proj_row(k, e):
        return rcopy(proj.at[k, z], proj.at[k, z], pjs.at[k], pjr.at[k], at_z(e))

    def core_sum(k):
        return rcopy(s1.at[k], r1.at[k], c1s.at[k], c1r.at[k], partner)

    def chip_sum(k, d):
        return rcopy(s2.at[k, d], r2.at[k, d], c2s.at[k], c2r.at[k], at_q(d))

    def slope_chip(k, d, slot):
        return rcopy(ST.at[k, slot], ST.at[k, slot], ags.at[k, d], agr.at[k, d], at_q(d))

    def slope_core(k, slot):
        return rcopy(ST.at[k, slot], ST.at[k, slot], ocs.at[k], ocr.at[k], partner)

    def back_row(k, e):
        return rcopy(sb.at[k, e], rs.at[k, e], bks.at[k], bkr.at[k], at_z(e))

    def weight_part(k, e, src, slot):
        return rcopy(wsend.at[k, src], wrecv.at[k, slot], wss.at[k], wsr.at[k], at_c(e))

    def weight_z(k, e, slot):
        return rcopy(zsum.at[k, slot], zsum.at[k, slot], zss.at[k], zsr.at[k], at_z(e))

    def weight_all(k, e, slot):
        return rcopy(fin.at[k, slot], fin.at[k, slot], fns.at[k], fnr.at[k], at_c(e))

    def proj_row_all(k):
        return rcopy(proj.at[k, pl.ds(0, R - 1)], proj.at[k, pl.ds(0, R - 1)], pjs.at[k], pjr.at[k], partner)

    def back_row_all(k):
        return rcopy(sb.at[k, pl.ds(0, R - 1)], rs.at[k, pl.ds(0, R - 1)], bks.at[k], bkr.at[k], partner)

    def chip_sum_all(k):
        return rcopy(s2.at[k, pl.ds(0, Q - 1)], r2.at[k, pl.ds(0, Q - 1)], c2s.at[k], c2r.at[k], partner)

    def slope_core_all(k):
        return rcopy(ST.at[k, pl.ds(0, Q)], ST.at[k, pl.ds(0, Q)], ocs.at[k], ocr.at[k], partner)

    def weight_part_group(k):
        return rcopy(wsend.at[k, pl.ds(0, C - 1)], wrecv.at[k, pl.ds(0, C - 1)], wss.at[k], wsr.at[k], partner)

    def weight_z_group(k):
        return rcopy(zsum.at[k, pl.ds(0, R - 1)], zsum.at[k, pl.ds(0, R - 1)], zss.at[k], zsr.at[k], partner)

    def weight_all_group(k):
        return rcopy(fin.at[k, pl.ds(0, C - 1)], fin.at[k, pl.ds(0, C - 1)], fns.at[k], fnr.at[k], partner)

    def cols(k):
        return pl.ds(pl.multiple_of(k * w, w), w)

    full = jnp.dot(feat[...], w_ref[...], preferred_element_type=jnp.float32).astype(jnp.bfloat16)
    for k in range(NCH):
        proj[k, z] = full[:, k * w:(k + 1) * w]
    pl.semaphore_wait(barrier, C + R - 2)

    def send_own(k):
        for e in range(1, R):
            proj_row(k, e).start()

    send_own(0)
    XT[...] = feat[...].astype(jnp.float32).T.astype(jnp.bfloat16)
    gacc[...] = jnp.zeros_like(gacc)
    adj_v[cap] = jnp.zeros((tile, tile), jnp.bfloat16)
    adj_copy.wait()

    @pl.loop(0, C * K)
    def _(rb):
        for cb in range(R * K):
            A[pl.ds(pl.multiple_of(rb * tile, tile), tile), cb * tile:(cb + 1) * tile] = adj_v[
                inv[rb * (R * K) + cb]
            ]

    def forward(k):
        proj_row_all(k).wait_recv()
        source = proj[k].reshape(R * B, w)

        def rows_of(c2):
            return A[pl.ds(pl.multiple_of(c2 * B, B), B), :]

        @pl.loop(0, Q)
        def _(j):
            s1[k, j] = jnp.dot(
                rows_of(2 * j + 1 - core), source, preferred_element_type=jnp.float32
            ).astype(jnp.bfloat16)

        core_sum(k).start()

        @pl.loop(0, Q)
        def _(j):
            p1[k, j] = jnp.dot(rows_of(2 * j + core), source, preferred_element_type=jnp.float32)

    def chip_send(k):
        core_sum(k).wait_recv()
        for d in range(1, Q):
            j = lax.rem(q + d, Q)
            s2[k, d] = (p1[k, j] + r1[k, j].astype(jnp.float32)).astype(jnp.bfloat16)
            chip_sum(k, d).start()

    def activate(k):
        total = p1[k, q] + r1[k, q].astype(jnp.float32)
        chip_sum_all(k).wait_recv()
        for d in range(1, Q):
            total = total + r2[k, d].astype(jnp.float32)
        shifted = total + bias[:, cols(k)]
        sig = jax.nn.sigmoid(shifted)
        slope = cot[:, cols(k)].astype(jnp.float32) * sig * (1.0 + shifted * (1.0 - sig))
        slope = slope.astype(jnp.bfloat16).astype(jnp.float32)
        ST[k, c] = slope.T.astype(jnp.bfloat16)
        for d in range(1, Q):
            slope_chip(k, d, c).start()
        slope_core(k, c).start()
        act[:, cols(k)] = (shifted * sig).astype(jnp.bfloat16)
        bp[k] = jnp.sum(slope, axis=0, keepdims=True)

    def slope_pass(k):
        for d in range(1, Q):
            slot = lax.rem(q - d + Q, Q) * 2 + core
            slope_chip(k, d, slot).wait_recv()
            slope_core(k, slot).start()

    def backward(k):
        slope_core_all(k).wait_recv()

        def piece(t):
            acc = jnp.zeros((w, B), jnp.float32)
            for j in range(C):
                acc = acc + jnp.dot(
                    ST[k, j],
                    A[j * B:(j + 1) * B, pl.ds(pl.multiple_of(t * B, B), B)],
                    preferred_element_type=jnp.float32,
                )
            return acc

        @pl.loop(1, R)
        def _(e):
            sb[k, e] = piece(lax.rem(z + e, R)).astype(jnp.bfloat16)
            back_row(k, e).start()

        pc[k] = piece(z)

    def finish(k):
        back_row_all(k).wait_recv()
        total = pc[k]
        for e in range(1, R):
            total = total + rs[k, e].astype(jnp.float32)
        back = total.T.astype(jnp.bfloat16)
        part = jnp.dot(XT[...], back, preferred_element_type=jnp.float32)
        wsend[k, :, 0:RW, :] = part.astype(jnp.bfloat16).reshape(C, RW, w)
        wsend[k, :, RW:RW + 16, :] = jnp.broadcast_to(bp[k].astype(jnp.bfloat16)[None], (C, 16, w))
        for e in range(1, C):
            weight_part(k, e, lax.rem(c + e, C), c).start()
        wrecv[k, c] = wsend[k, c]
        gacc[...] += lax.dot_general(
            back, w_ref[:, cols(k)], (((1,), (1,)), ((), ())), preferred_element_type=jnp.float32
        )

        @pl.when(k == NCH - 1)
        def _():
            gin[...] = gacc[...].astype(jnp.bfloat16)

    def weight_sum(k):
        weight_part_group(k).wait_recv()
        total = wrecv[k, 0].astype(jnp.float32)
        for j in range(1, C):
            total = total + wrecv[k, j].astype(jnp.float32)
        zsum[k, z] = total.astype(jnp.bfloat16)
        for e in range(1, R):
            weight_z(k, e, z).start()

    def weight_total(k):
        weight_z_group(k).wait_recv()
        total = zsum[k, 0].astype(jnp.float32)
        for j in range(1, R):
            total = total + zsum[k, j].astype(jnp.float32)
        total = total * scale
        fin[k, c] = total[0:RW].astype(jnp.bfloat16)
        for e in range(1, C):
            weight_all(k, e, c).start()
        gb[:, cols(k)] = total[RW:RW + 1]

    def weight_out(k):
        weight_all_group(k).wait_recv()
        gw[:, cols(k)] = fin[k].reshape(F, w)

    stages = [
        (4, finish),
        (3, slope_pass),
        (2, activate),
        (1, chip_send),
        (3, backward),
        (0, forward),
        (7, weight_out),
        (6, weight_total),
        (5, weight_sum),
    ]

    @pl.loop(0, NCH + 7)
    def _(i):
        @pl.when(i + 1 < NCH)
        def _():
            send_own(i + 1)

        for after, stage in stages:
            at = i - after

            @pl.when((at >= 0) & (at < NCH))
            def _():
                stage(at)

    @pl.loop(0, NCH)
    def _(k):
        proj_row_all(k).wait_send()
        core_sum(k).wait_send()
        chip_sum_all(k).wait_send()
        for d in range(1, Q):
            slope_chip(k, d, c).wait_send()
        slope_core_all(k).wait_send()
        back_row_all(k).wait_send()
        weight_part_group(k).wait_send()
        weight_z_group(k).wait_send()
        weight_all_group(k).wait_send()


def on_device(R, C, features, cotangent, weights, bias_term, adjacency, tile_rows, tile_cols, tile_count):
    tile = adjacency.shape[-1]
    cap = adjacency.shape[2]
    B, F = features.shape
    K = B // tile
    Q = C // 2
    w = F // NCH
    RW = F // C
    pairs = C * K * R * K
    slots = jnp.arange(cap, dtype=jnp.int32)
    pair = tile_rows.reshape(cap) * (R * K) + tile_cols.reshape(cap)
    pair = jnp.where(slots < tile_count.reshape(()), pair, -1)
    hit = jnp.arange(pairs, dtype=jnp.int32)[:, None] == pair[None, :]
    inv = cap + jnp.sum(jnp.where(hit, slots[None, :] - cap, 0), axis=1, dtype=jnp.int32)
    bf, f32 = jnp.bfloat16, jnp.float32
    vmem = pl.BlockSpec(memory_space=pltpu.VMEM)
    V = pltpu.VMEM

    group = pltpu.SemaphoreType.DMA((NCH,))

    def sems(n):
        return pltpu.SemaphoreType.DMA((NCH, n))

    act, gin, gw, gb = pl.pallas_call(
        functools.partial(kernel, R, C, tile, cap, 1.0 / math.sqrt(B * R * C)),
        out_shape=(
            jax.ShapeDtypeStruct((B, F), bf),
            jax.ShapeDtypeStruct((B, F), bf),
            jax.ShapeDtypeStruct((F, F), bf),
            jax.ShapeDtypeStruct((1, F), f32),
        ),
        in_specs=[vmem] * 4 + [pl.BlockSpec(memory_space=pltpu.SMEM), pl.BlockSpec(memory_space=pl.ANY)],
        out_specs=(vmem,) * 4,
        scratch_shapes=[
            V((cap + 1, tile, tile), bf),
            V((C * B, R * B), bf),
            V((NCH, R, B, w), bf),
            V((NCH, Q, B, w), bf),
            V((NCH, Q, B, w), bf),
            V((NCH, Q, B, w), f32),
            V((NCH, Q, B, w), bf),
            V((NCH, Q, B, w), bf),
            V((NCH, C, w, B), bf),
            V((NCH, w, B), f32),
            V((NCH, R, w, B), bf),
            V((NCH, R, w, B), bf),
            V((F, B), bf),
            V((NCH, 1, w), f32),
            V((B, F), f32),
            V((NCH, C, RW + 16, w), bf),
            V((NCH, C, RW + 16, w), bf),
            V((NCH, R, RW + 16, w), bf),
            V((NCH, C, RW, w), bf),
            pltpu.SemaphoreType.DMA,
            group, group,
            group, group,
            group, group, sems(Q), sems(Q), group, group,
            group, group,
            group, group, group, group, group, group,
        ],
        compiler_params=pltpu.CompilerParams(
            collective_id=0, has_side_effects=True, vmem_limit_bytes=60 * 1024 * 1024
        ),
    )(features, cotangent, weights, bias_term[None, :], inv, adjacency.reshape(cap, tile, tile))
    return act, gin, gw.astype(f32), gb.reshape(F)


def solution(mesh):
    return jax.shard_map(
        functools.partial(on_device, mesh.shape["row"], mesh.shape["col"]),
        mesh=mesh,
        in_specs=(
            P(("row", "col"), None),
            P(("row", "col"), None),
            P(),
            P(),
            P("row", "col", None, None, None),
            P("row", "col", None),
            P("row", "col", None),
            P("row", "col"),
        ),
        out_specs=(P(("row", "col"), None), P(("row", "col"), None), P(), P()),
        check_vma=False,
    )
```

```python
import functools
import math

import jax
import jax.numpy as jnp
from jax import lax
from jax.experimental import pallas as pl
from jax.experimental.pallas import tpu as pltpu
from jax.sharding import PartitionSpec as P

MESH = pl.DeviceIdType.MESH
NCH = 4


def kernel(
    R, C, tile, cap, scale,
    feat, cot, w_ref, bias, inv, adj_hbm,
    act, gin, gw, gb,
    adj_v, A, proj, s1, r1, p1, s2, r2, ST, pc, sb, rs, XT, bp, gacc,
    wsend, wrecv, zsum, fin,
    adj_sem, pjs, pjr, c1s, c1r, c2s, c2r, ags, agr, ocs, ocr,
    bks, bkr, wss, wsr, zss, zsr, fns, fnr,
):
    B, F = feat.shape
    w = F // NCH
    Q = C // 2
    RW = F // C
    K = B // tile
    z = lax.axis_index("row")
    c = lax.axis_index("col")
    core = lax.rem(c, 2)
    q = c // 2
    partner = (z, q * 2 + 1 - core)

    def at_q(d):
        return (z, lax.rem(q + d, Q) * 2 + core)

    def at_c(e):
        return (z, lax.rem(c + e, C))

    def at_z(e):
        return (lax.rem(z + e, R), c)

    adj_copy = pltpu.make_async_copy(adj_hbm, adj_v.at[pl.ds(0, cap)], adj_sem)
    adj_copy.start()

    barrier = pltpu.get_barrier_semaphore()
    for e in range(1, C):
        pl.semaphore_signal(barrier, inc=1, device_id=at_c(e), device_id_type=MESH)
    for e in range(1, R):
        pl.semaphore_signal(barrier, inc=1, device_id=at_z(e), device_id_type=MESH)

    def rcopy(src, dst, ss, rs, dev):
        return pltpu.make_async_remote_copy(
            src_ref=src, dst_ref=dst, send_sem=ss, recv_sem=rs, device_id=dev, device_id_type=MESH
        )

    def proj_row(k, e):
        return rcopy(proj.at[k, z], proj.at[k, z], pjs.at[k], pjr.at[k], at_z(e))

    def core_sum(k):
        return rcopy(s1.at[k], r1.at[k], c1s.at[k], c1r.at[k], partner)

    def chip_sum(k, d):
        return rcopy(s2.at[k, d], r2.at[k, d], c2s.at[k], c2r.at[k], at_q(d))

    def slope_chip(k, d, slot):
        return rcopy(ST.at[k, slot], ST.at[k, slot], ags.at[k, d], agr.at[k, d], at_q(d))

    def slope_core(k, slot):
        return rcopy(ST.at[k, slot], ST.at[k, slot], ocs.at[k], ocr.at[k], partner)

    def back_row(k, e):
        return rcopy(sb.at[k, e], rs.at[k, e], bks.at[k], bkr.at[k], at_z(e))

    def weight_part(k, e, src, slot):
        return rcopy(wsend.at[k, src], wrecv.at[k, slot], wss.at[k], wsr.at[k], at_c(e))

    def weight_z(k, e, slot):
        return rcopy(zsum.at[k, slot], zsum.at[k, slot], zss.at[k], zsr.at[k], at_z(e))

    def weight_all(k, e, slot):
        return rcopy(fin.at[k, slot], fin.at[k, slot], fns.at[k], fnr.at[k], at_c(e))

    def proj_row_all(k):
        return rcopy(proj.at[k, pl.ds(0, R - 1)], proj.at[k, pl.ds(0, R - 1)], pjs.at[k], pjr.at[k], partner)

    def back_row_all(k):
        return rcopy(sb.at[k, pl.ds(0, R - 1)], rs.at[k, pl.ds(0, R - 1)], bks.at[k], bkr.at[k], partner)

    def chip_sum_all(k):
        return rcopy(s2.at[k, pl.ds(0, Q - 1)], r2.at[k, pl.ds(0, Q - 1)], c2s.at[k], c2r.at[k], partner)

    def slope_core_all(k):
        return rcopy(ST.at[k, pl.ds(0, Q)], ST.at[k, pl.ds(0, Q)], ocs.at[k], ocr.at[k], partner)

    def weight_part_group(k):
        return rcopy(wsend.at[k, pl.ds(0, C - 1)], wrecv.at[k, pl.ds(0, C - 1)], wss.at[k], wsr.at[k], partner)

    def weight_z_group(k):
        return rcopy(zsum.at[k, pl.ds(0, R - 1)], zsum.at[k, pl.ds(0, R - 1)], zss.at[k], zsr.at[k], partner)

    def weight_all_group(k):
        return rcopy(fin.at[k, pl.ds(0, C - 1)], fin.at[k, pl.ds(0, C - 1)], fns.at[k], fnr.at[k], partner)

    def cols(k):
        return pl.ds(pl.multiple_of(k * w, w), w)

    full = jnp.dot(feat[...], w_ref[...], preferred_element_type=jnp.float32).astype(jnp.bfloat16)
    for k in range(NCH):
        proj[k, z] = full[:, k * w:(k + 1) * w]
    pl.semaphore_wait(barrier, C + R - 2)

    def send_own(k):
        for e in range(1, R):
            proj_row(k, e).start()

    send_own(0)
    XT[...] = feat[...].astype(jnp.float32).T.astype(jnp.bfloat16)
    gacc[...] = jnp.zeros_like(gacc)
    adj_v[cap] = jnp.zeros((tile, tile), jnp.bfloat16)
    adj_copy.wait()

    @pl.loop(0, C * K)
    def _(rb):
        for cb in range(R * K):
            A[pl.ds(pl.multiple_of(rb * tile, tile), tile), cb * tile:(cb + 1) * tile] = adj_v[
                inv[rb * (R * K) + cb]
            ]

    def forward(k):
        proj_row_all(k).wait_recv()
        source = proj[k].reshape(R * B, w)

        def rows_of(c2):
            return A[pl.ds(pl.multiple_of(c2 * B, B), B), :]

        @pl.loop(0, Q)
        def _(j):
            s1[k, j] = jnp.dot(
                rows_of(2 * j + 1 - core), source, preferred_element_type=jnp.float32
            ).astype(jnp.bfloat16)

        core_sum(k).start()

        @pl.loop(0, Q)
        def _(j):
            p1[k, j] = jnp.dot(rows_of(2 * j + core), source, preferred_element_type=jnp.float32)

    def chip_send(k):
        core_sum(k).wait_recv()
        for d in range(1, Q):
            j = lax.rem(q + d, Q)
            s2[k, d] = (p1[k, j] + r1[k, j].astype(jnp.float32)).astype(jnp.bfloat16)
            chip_sum(k, d).start()

    def activate(k):
        total = p1[k, q] + r1[k, q].astype(jnp.float32)
        chip_sum_all(k).wait_recv()
        for d in range(1, Q):
            total = total + r2[k, d].astype(jnp.float32)
        shifted = total + bias[:, cols(k)]
        sig = jax.nn.sigmoid(shifted)
        slope = cot[:, cols(k)].astype(jnp.float32) * sig * (1.0 + shifted * (1.0 - sig))
        slope = slope.astype(jnp.bfloat16).astype(jnp.float32)
        ST[k, c] = slope.T.astype(jnp.bfloat16)
        for d in range(1, Q):
            slope_chip(k, d, c).start()
        slope_core(k, c).start()
        act[:, cols(k)] = (shifted * sig).astype(jnp.bfloat16)
        bp[k] = jnp.sum(slope, axis=0, keepdims=True)

    def slope_pass(k):
        for d in range(1, Q):
            slot = lax.rem(q - d + Q, Q) * 2 + core
            slope_chip(k, d, slot).wait_recv()
            slope_core(k, slot).start()

    def backward(k):
        slope_core_all(k).wait_recv()

        def piece(t):
            return jnp.dot(
                jnp.concatenate([ST[k, j] for j in range(C)], axis=1),
                A[:, pl.ds(pl.multiple_of(t * B, B), B)],
                preferred_element_type=jnp.float32,
            )

        @pl.loop(1, R)
        def _(e):
            sb[k, e] = piece(lax.rem(z + e, R)).astype(jnp.bfloat16)
            back_row(k, e).start()

        pc[k] = piece(z)

    def finish(k):
        back_row_all(k).wait_recv()
        total = pc[k]
        for e in range(1, R):
            total = total + rs[k, e].astype(jnp.float32)
        back = total.T.astype(jnp.bfloat16)
        part = jnp.dot(XT[...], back, preferred_element_type=jnp.float32)
        wsend[k, :, 0:RW, :] = part.astype(jnp.bfloat16).reshape(C, RW, w)
        wsend[k, :, RW:RW + 16, :] = jnp.broadcast_to(bp[k].astype(jnp.bfloat16)[None], (C, 16, w))
        for e in range(1, C):
            weight_part(k, e, lax.rem(c + e, C), c).start()
        wrecv[k, c] = wsend[k, c]
        gacc[...] += lax.dot_general(
            back, w_ref[:, cols(k)], (((1,), (1,)), ((), ())), preferred_element_type=jnp.float32
        )

        @pl.when(k == NCH - 1)
        def _():
            gin[...] = gacc[...].astype(jnp.bfloat16)

    def weight_sum(k):
        weight_part_group(k).wait_recv()
        total = wrecv[k, 0].astype(jnp.float32)
        for j in range(1, C):
            total = total + wrecv[k, j].astype(jnp.float32)
        zsum[k, z] = total.astype(jnp.bfloat16)
        for e in range(1, R):
            weight_z(k, e, z).start()

    def weight_total(k):
        weight_z_group(k).wait_recv()
        total = zsum[k, 0].astype(jnp.float32)
        for j in range(1, R):
            total = total + zsum[k, j].astype(jnp.float32)
        total = total * scale
        fin[k, c] = total[0:RW].astype(jnp.bfloat16)
        for e in range(1, C):
            weight_all(k, e, c).start()
        gb[:, cols(k)] = total[RW:RW + 1]

    def weight_out(k):
        weight_all_group(k).wait_recv()
        gw[:, cols(k)] = fin[k].reshape(F, w)

    stages = [
        (3, slope_pass),
        (2, activate),
        (1, chip_send),
        (3, backward),
        (0, forward),
        (4, finish),
        (7, weight_out),
        (6, weight_total),
        (5, weight_sum),
    ]

    @pl.loop(0, NCH + 7)
    def _(i):
        @pl.when(i + 1 < NCH)
        def _():
            send_own(i + 1)

        for after, stage in stages:
            at = i - after

            @pl.when((at >= 0) & (at < NCH))
            def _():
                stage(at)

    @pl.loop(0, NCH)
    def _(k):
        proj_row_all(k).wait_send()
        core_sum(k).wait_send()
        chip_sum_all(k).wait_send()
        for d in range(1, Q):
            slope_chip(k, d, c).wait_send()
        slope_core_all(k).wait_send()
        back_row_all(k).wait_send()
        weight_part_group(k).wait_send()
        weight_z_group(k).wait_send()
        weight_all_group(k).wait_send()


def on_device(R, C, features, cotangent, weights, bias_term, adjacency, tile_rows, tile_cols, tile_count):
    tile = adjacency.shape[-1]
    cap = adjacency.shape[2]
    B, F = features.shape
    K = B // tile
    Q = C // 2
    w = F // NCH
    RW = F // C
    pairs = C * K * R * K
    slots = jnp.arange(cap, dtype=jnp.int32)
    pair = tile_rows.reshape(cap) * (R * K) + tile_cols.reshape(cap)
    pair = jnp.where(slots < tile_count.reshape(()), pair, -1)
    hit = jnp.arange(pairs, dtype=jnp.int32)[:, None] == pair[None, :]
    inv = cap + jnp.sum(jnp.where(hit, slots[None, :] - cap, 0), axis=1, dtype=jnp.int32)
    bf, f32 = jnp.bfloat16, jnp.float32
    vmem = pl.BlockSpec(memory_space=pltpu.VMEM)
    V = pltpu.VMEM

    group = pltpu.SemaphoreType.DMA((NCH,))

    def sems(n):
        return pltpu.SemaphoreType.DMA((NCH, n))

    act, gin, gw, gb = pl.pallas_call(
        functools.partial(kernel, R, C, tile, cap, 1.0 / math.sqrt(B * R * C)),
        out_shape=(
            jax.ShapeDtypeStruct((B, F), bf),
            jax.ShapeDtypeStruct((B, F), bf),
            jax.ShapeDtypeStruct((F, F), bf),
            jax.ShapeDtypeStruct((1, F), f32),
        ),
        in_specs=[vmem] * 4 + [pl.BlockSpec(memory_space=pltpu.SMEM), pl.BlockSpec(memory_space=pl.ANY)],
        out_specs=(vmem,) * 4,
        scratch_shapes=[
            V((cap + 1, tile, tile), bf),
            V((C * B, R * B), bf),
            V((NCH, R, B, w), bf),
            V((NCH, Q, B, w), bf),
            V((NCH, Q, B, w), bf),
            V((NCH, Q, B, w), f32),
            V((NCH, Q, B, w), bf),
            V((NCH, Q, B, w), bf),
            V((NCH, C, w, B), bf),
            V((NCH, w, B), f32),
            V((NCH, R, w, B), bf),
            V((NCH, R, w, B), bf),
            V((F, B), bf),
            V((NCH, 1, w), f32),
            V((B, F), f32),
            V((NCH, C, RW + 16, w), bf),
            V((NCH, C, RW + 16, w), bf),
            V((NCH, R, RW + 16, w), bf),
            V((NCH, C, RW, w), bf),
            pltpu.SemaphoreType.DMA,
            group, group,
            group, group,
            group, group, sems(Q), sems(Q), group, group,
            group, group,
            group, group, group, group, group, group,
        ],
        compiler_params=pltpu.CompilerParams(
            collective_id=0, has_side_effects=True, vmem_limit_bytes=60 * 1024 * 1024
        ),
    )(features, cotangent, weights, bias_term[None, :], inv, adjacency.reshape(cap, tile, tile))
    return act, gin, gw.astype(f32), gb.reshape(F)


def solution(mesh):
    return jax.shard_map(
        functools.partial(on_device, mesh.shape["row"], mesh.shape["col"]),
        mesh=mesh,
        in_specs=(
            P(("row", "col"), None),
            P(("row", "col"), None),
            P(),
            P(),
            P("row", "col", None, None, None),
            P("row", "col", None),
            P("row", "col", None),
            P("row", "col"),
        ),
        out_specs=(P(("row", "col"), None), P(("row", "col"), None), P(), P()),
        check_vma=False,
    )
```

```python
import functools
import math

import jax
import jax.numpy as jnp
from jax import lax
from jax.experimental import pallas as pl
from jax.experimental.pallas import tpu as pltpu
from jax.sharding import PartitionSpec as P

MESH = pl.DeviceIdType.MESH
NCH = 4


def kernel(
    R, C, tile, cap, scale,
    feat, cot, w_ref, bias, inv, adj_hbm,
    act, gin, gw, gb,
    adj_v, A, proj, s1, r1, p1, s2, r2, ST, pc, sb, rs, XT, bp, gacc,
    wsend, wrecv, zsum, fin,
    adj_sem, pjs, pjr, c1s, c1r, c2s, c2r, ags, agr, ocs, ocr,
    bks, bkr, wss, wsr, zss, zsr, fns, fnr,
):
    B, F = feat.shape
    w = F // NCH
    Q = C // 2
    RW = F // C
    K = B // tile
    z = lax.axis_index("row")
    c = lax.axis_index("col")
    core = lax.rem(c, 2)
    q = c // 2
    partner = (z, q * 2 + 1 - core)

    def at_q(d):
        return (z, lax.rem(q + d, Q) * 2 + core)

    def at_c(e):
        return (z, lax.rem(c + e, C))

    def at_z(e):
        return (lax.rem(z + e, R), c)

    adj_copy = pltpu.make_async_copy(adj_hbm, adj_v.at[pl.ds(0, cap)], adj_sem)
    adj_copy.start()

    barrier = pltpu.get_barrier_semaphore()
    for e in range(1, C):
        pl.semaphore_signal(barrier, inc=1, device_id=at_c(e), device_id_type=MESH)
    for e in range(1, R):
        pl.semaphore_signal(barrier, inc=1, device_id=at_z(e), device_id_type=MESH)

    def rcopy(src, dst, ss, rs, dev):
        return pltpu.make_async_remote_copy(
            src_ref=src, dst_ref=dst, send_sem=ss, recv_sem=rs, device_id=dev, device_id_type=MESH
        )

    def proj_row(k, e):
        return rcopy(proj.at[k, z], proj.at[k, z], pjs.at[k], pjr.at[k], at_z(e))

    def core_sum(k):
        return rcopy(s1.at[k], r1.at[k], c1s.at[k], c1r.at[k], partner)

    def chip_sum(k, d):
        return rcopy(s2.at[k, d], r2.at[k, d], c2s.at[k], c2r.at[k], at_q(d))

    def slope_chip(k, d, slot):
        return rcopy(ST.at[k, slot], ST.at[k, slot], ags.at[k, d], agr.at[k, d], at_q(d))

    def slope_core(k, slot):
        return rcopy(ST.at[k, slot], ST.at[k, slot], ocs.at[k], ocr.at[k], partner)

    def back_row(k, e):
        return rcopy(sb.at[k, e], rs.at[k, e], bks.at[k], bkr.at[k], at_z(e))

    def weight_part(k, e, src, slot):
        return rcopy(wsend.at[k, src], wrecv.at[k, slot], wss.at[k], wsr.at[k], at_c(e))

    def weight_z(k, e, slot):
        return rcopy(zsum.at[k, slot], zsum.at[k, slot], zss.at[k], zsr.at[k], at_z(e))

    def weight_all(k, e, slot):
        return rcopy(fin.at[k, slot], fin.at[k, slot], fns.at[k], fnr.at[k], at_c(e))

    def proj_row_all(k):
        return rcopy(proj.at[k, pl.ds(0, R - 1)], proj.at[k, pl.ds(0, R - 1)], pjs.at[k], pjr.at[k], partner)

    def back_row_all(k):
        return rcopy(sb.at[k, pl.ds(0, R - 1)], rs.at[k, pl.ds(0, R - 1)], bks.at[k], bkr.at[k], partner)

    def chip_sum_all(k):
        return rcopy(s2.at[k, pl.ds(0, Q - 1)], r2.at[k, pl.ds(0, Q - 1)], c2s.at[k], c2r.at[k], partner)

    def slope_core_all(k):
        return rcopy(ST.at[k, pl.ds(0, Q)], ST.at[k, pl.ds(0, Q)], ocs.at[k], ocr.at[k], partner)

    def weight_part_group(k):
        return rcopy(wsend.at[k, pl.ds(0, C - 1)], wrecv.at[k, pl.ds(0, C - 1)], wss.at[k], wsr.at[k], partner)

    def weight_z_group(k):
        return rcopy(zsum.at[k, pl.ds(0, R - 1)], zsum.at[k, pl.ds(0, R - 1)], zss.at[k], zsr.at[k], partner)

    def weight_all_group(k):
        return rcopy(fin.at[k, pl.ds(0, C - 1)], fin.at[k, pl.ds(0, C - 1)], fns.at[k], fnr.at[k], partner)

    def cols(k):
        return pl.ds(pl.multiple_of(k * w, w), w)

    full = jnp.dot(feat[...], w_ref[...], preferred_element_type=jnp.float32).astype(jnp.bfloat16)
    for k in range(NCH):
        proj[k, z] = full[:, k * w:(k + 1) * w]
    pl.semaphore_wait(barrier, C + R - 2)

    def send_own(k):
        for e in range(1, R):
            proj_row(k, e).start()

    send_own(0)
    XT[...] = feat[...].astype(jnp.float32).T.astype(jnp.bfloat16)
    gacc[...] = jnp.zeros_like(gacc)
    send_own(1)
    adj_v[cap] = jnp.zeros((tile, tile), jnp.bfloat16)
    adj_copy.wait()

    @pl.loop(0, C * K)
    def _(rb):
        for cb in range(R * K):
            A[pl.ds(pl.multiple_of(rb * tile, tile), tile), cb * tile:(cb + 1) * tile] = adj_v[
                inv[rb * (R * K) + cb]
            ]

    def forward(k):
        proj_row_all(k).wait_recv()
        source = proj[k].reshape(R * B, w)

        def rows_of(c2):
            return A[pl.ds(pl.multiple_of(c2 * B, B), B), :]

        @pl.loop(0, Q)
        def _(j):
            s1[k, j] = jnp.dot(
                rows_of(2 * j + 1 - core), source, preferred_element_type=jnp.float32
            ).astype(jnp.bfloat16)

        core_sum(k).start()

        @pl.loop(0, Q)
        def _(j):
            p1[k, j] = jnp.dot(rows_of(2 * j + core), source, preferred_element_type=jnp.float32)

    def chip_send(k):
        core_sum(k).wait_recv()
        for d in range(1, Q):
            j = lax.rem(q + d, Q)
            s2[k, d] = (p1[k, j] + r1[k, j].astype(jnp.float32)).astype(jnp.bfloat16)
            chip_sum(k, d).start()

    def activate(k):
        total = p1[k, q] + r1[k, q].astype(jnp.float32)
        chip_sum_all(k).wait_recv()
        for d in range(1, Q):
            total = total + r2[k, d].astype(jnp.float32)
        shifted = total + bias[:, cols(k)]
        sig = jax.nn.sigmoid(shifted)
        slope = cot[:, cols(k)].astype(jnp.float32) * sig * (1.0 + shifted * (1.0 - sig))
        slope = slope.astype(jnp.bfloat16).astype(jnp.float32)
        ST[k, c] = slope.T.astype(jnp.bfloat16)
        for d in range(1, Q):
            slope_chip(k, d, c).start()
        slope_core(k, c).start()
        act[:, cols(k)] = (shifted * sig).astype(jnp.bfloat16)
        bp[k] = jnp.sum(slope, axis=0, keepdims=True)

    def slope_pass(k):
        for d in range(1, Q):
            slot = lax.rem(q - d + Q, Q) * 2 + core
            slope_chip(k, d, slot).wait_recv()
            slope_core(k, slot).start()

    def backward(k):
        slope_core_all(k).wait_recv()

        def piece(t):
            return jnp.dot(
                jnp.concatenate([ST[k, j] for j in range(C)], axis=1),
                A[:, pl.ds(pl.multiple_of(t * B, B), B)],
                preferred_element_type=jnp.float32,
            )

        @pl.loop(1, R)
        def _(e):
            sb[k, e] = piece(lax.rem(z + e, R)).astype(jnp.bfloat16)
            back_row(k, e).start()

        pc[k] = piece(z)

    def finish(k):
        back_row_all(k).wait_recv()
        total = pc[k]
        for e in range(1, R):
            total = total + rs[k, e].astype(jnp.float32)
        back = total.T.astype(jnp.bfloat16)
        part = jnp.dot(XT[...], back, preferred_element_type=jnp.float32)
        wsend[k, :, 0:RW, :] = part.astype(jnp.bfloat16).reshape(C, RW, w)
        wsend[k, :, RW:RW + 16, :] = jnp.broadcast_to(bp[k].astype(jnp.bfloat16)[None], (C, 16, w))
        for e in range(1, C):
            weight_part(k, e, lax.rem(c + e, C), c).start()
        wrecv[k, c] = wsend[k, c]
        gacc[...] += lax.dot_general(
            back, w_ref[:, cols(k)], (((1,), (1,)), ((), ())), preferred_element_type=jnp.float32
        )

        @pl.when(k == NCH - 1)
        def _():
            gin[...] = gacc[...].astype(jnp.bfloat16)

    def weight_sum(k):
        weight_part_group(k).wait_recv()
        total = wrecv[k, 0].astype(jnp.float32)
        for j in range(1, C):
            total = total + wrecv[k, j].astype(jnp.float32)
        zsum[k, z] = total.astype(jnp.bfloat16)
        for e in range(1, R):
            weight_z(k, e, z).start()

    def weight_total(k):
        weight_z_group(k).wait_recv()
        total = zsum[k, 0].astype(jnp.float32)
        for j in range(1, R):
            total = total + zsum[k, j].astype(jnp.float32)
        total = total * scale
        fin[k, c] = total[0:RW].astype(jnp.bfloat16)
        for e in range(1, C):
            weight_all(k, e, c).start()
        gb[:, cols(k)] = total[RW:RW + 1]

    def weight_out(k):
        weight_all_group(k).wait_recv()
        gw[:, cols(k)] = fin[k].reshape(F, w)

    stages = [
        (3, slope_pass),
        (2, activate),
        (1, chip_send),
        (3, backward),
        (0, forward),
        (4, finish),
        (7, weight_out),
        (6, weight_total),
        (5, weight_sum),
    ]

    @pl.loop(0, NCH + 7)
    def _(i):
        @pl.when(i + 2 < NCH)
        def _():
            send_own(i + 2)

        for after, stage in stages:
            at = i - after

            @pl.when((at >= 0) & (at < NCH))
            def _():
                stage(at)

    @pl.loop(0, NCH)
    def _(k):
        proj_row_all(k).wait_send()
        core_sum(k).wait_send()
        chip_sum_all(k).wait_send()
        for d in range(1, Q):
            slope_chip(k, d, c).wait_send()
        slope_core_all(k).wait_send()
        back_row_all(k).wait_send()
        weight_part_group(k).wait_send()
        weight_z_group(k).wait_send()
        weight_all_group(k).wait_send()


def on_device(R, C, features, cotangent, weights, bias_term, adjacency, tile_rows, tile_cols, tile_count):
    tile = adjacency.shape[-1]
    cap = adjacency.shape[2]
    B, F = features.shape
    K = B // tile
    Q = C // 2
    w = F // NCH
    RW = F // C
    pairs = C * K * R * K
    slots = jnp.arange(cap, dtype=jnp.int32)
    pair = tile_rows.reshape(cap) * (R * K) + tile_cols.reshape(cap)
    pair = jnp.where(slots < tile_count.reshape(()), pair, -1)
    hit = jnp.arange(pairs, dtype=jnp.int32)[:, None] == pair[None, :]
    inv = cap + jnp.sum(jnp.where(hit, slots[None, :] - cap, 0), axis=1, dtype=jnp.int32)
    bf, f32 = jnp.bfloat16, jnp.float32
    vmem = pl.BlockSpec(memory_space=pltpu.VMEM)
    V = pltpu.VMEM

    group = pltpu.SemaphoreType.DMA((NCH,))

    def sems(n):
        return pltpu.SemaphoreType.DMA((NCH, n))

    act, gin, gw, gb = pl.pallas_call(
        functools.partial(kernel, R, C, tile, cap, 1.0 / math.sqrt(B * R * C)),
        out_shape=(
            jax.ShapeDtypeStruct((B, F), bf),
            jax.ShapeDtypeStruct((B, F), bf),
            jax.ShapeDtypeStruct((F, F), bf),
            jax.ShapeDtypeStruct((1, F), f32),
        ),
        in_specs=[vmem] * 4 + [pl.BlockSpec(memory_space=pltpu.SMEM), pl.BlockSpec(memory_space=pl.ANY)],
        out_specs=(vmem,) * 4,
        scratch_shapes=[
            V((cap + 1, tile, tile), bf),
            V((C * B, R * B), bf),
            V((NCH, R, B, w), bf),
            V((NCH, Q, B, w), bf),
            V((NCH, Q, B, w), bf),
            V((NCH, Q, B, w), f32),
            V((NCH, Q, B, w), bf),
            V((NCH, Q, B, w), bf),
            V((NCH, C, w, B), bf),
            V((NCH, w, B), f32),
            V((NCH, R, w, B), bf),
            V((NCH, R, w, B), bf),
            V((F, B), bf),
            V((NCH, 1, w), f32),
            V((B, F), f32),
            V((NCH, C, RW + 16, w), bf),
            V((NCH, C, RW + 16, w), bf),
            V((NCH, R, RW + 16, w), bf),
            V((NCH, C, RW, w), bf),
            pltpu.SemaphoreType.DMA,
            group, group,
            group, group,
            group, group, sems(Q), sems(Q), group, group,
            group, group,
            group, group, group, group, group, group,
        ],
        compiler_params=pltpu.CompilerParams(
            collective_id=0, has_side_effects=True, vmem_limit_bytes=60 * 1024 * 1024
        ),
    )(features, cotangent, weights, bias_term[None, :], inv, adjacency.reshape(cap, tile, tile))
    return act, gin, gw.astype(f32), gb.reshape(F)


def solution(mesh):
    return jax.shard_map(
        functools.partial(on_device, mesh.shape["row"], mesh.shape["col"]),
        mesh=mesh,
        in_specs=(
            P(("row", "col"), None),
            P(("row", "col"), None),
            P(),
            P(),
            P("row", "col", None, None, None),
            P("row", "col", None),
            P("row", "col", None),
            P("row", "col"),
        ),
        out_specs=(P(("row", "col"), None), P(("row", "col"), None), P(), P()),
        check_vma=False,
    )
```
